128 devices in a mesh: az: 4 (over y), rg: 32 (over x, z, core).
Axes of the slice: x: 4, y: 4, z: 4, core: 2. Of those that a mesh axis runs over, the one named last changes fastest.
Arguments:
- echoes: bfloat16 [2, 8, 512, 8192], P(None, None, ('az', 'rg')), may hold values from -6 to 6
- replica: float32 [2, 8192], replicated, may hold values from -6 to 6
- filter_bank: bfloat16 [2, 8, 8, 256], replicated, may hold values from -2 to 2
- doppler_rate: float32 [8192], P('rg'), may hold values from 20 to 400
- doppler_width: int32 [8192], P('rg'), may hold values from 512 to 1024
- migration: int32 [8192], P('rg'), may hold values from 0 to 32, as said below
Outputs:
- focused: bfloat16 [2, 4096, 8192], P(None, 'az', 'rg')
The draws below stay inside these ranges and needn't reach their ends.
Inputs may be any that keep to these rules, and one draw needn't show every extreme that they name: Some range bin has migration 32.
All inputs are finite; a program needn't handle non-finite values.
Results may differ from the reference program's by a relative error of at most 0.02.
Values may be sent and summed in bfloat16 or wider, within the bound.
A program may use at most 128 MiB of HBM per device.

```python
import math
import jax
import jax.numpy as jnp
from jax import lax

CH = 8
RA = 128
RB = 64
R = 8192
PULSES = 512
E = 64
M = 256
MB = 32
OV = 32
N_AZ = 4
N_RG = 32


def draw_migration(key, part):
    key = jax.random.fold_in(key, 7)
    values = jax.random.randint(key, (R,), 0, OV + 1)
    block_width = R // N_RG
    rim_bins = max(OV // 4, 1)
    bins = jnp.arange(R, dtype=jnp.int32)
    at_rim = bins % block_width >= block_width - rim_bins
    return jnp.where(at_rim, OV, values).astype(jnp.int32)


def plant(array, rng, low, high):
    longest = array.shape.index(max(array.shape))
    spots = []
    for shift in (0, 1):
        where = [jax.random.randint(jax.random.fold_in(rng, axis), (), 0, length) for axis, length in enumerate(array.shape)]
        where[longest] = (where[longest] + shift) % array.shape[longest]
        spots.append(tuple(where))
    return array.at[spots[0]].set(low).at[spots[1]].set(high)


def block_levels(own_key, dims, cuts, least, top_value):
    loudness, own = 1.0, jax.random.fold_in(own_key, 6)
    for position, blocks in cuts:
        draws = jnp.exp(jax.random.uniform(jax.random.fold_in(own, position), (blocks,), jnp.float32, least / len(cuts), top_value / len(cuts)))
        loudness = loudness * jnp.repeat(draws, dims[position] // blocks).reshape([-1 if axis == position else 1 for axis in range(len(dims))])
    return loudness


def centred(key, dims, scale, reach, cuts=(), held_as=jnp.bfloat16):
    loudness = block_levels(key, dims, cuts, -0.22, 0.18) if cuts else 1.0
    values = jax.random.normal(key, dims, jnp.float32) * scale * loudness
    return jnp.minimum(jnp.maximum(values, -reach), reach).astype(held_as)


def setup_inputs(seed: int = 0) -> dict:
    arg_keys = jax.random.split(jax.random.key(seed), 7)
    return {
        "echoes": centred(arg_keys[0], (2, CH, PULSES, R), 1.0, 6.0, ((2, 128),)),
        "replica": centred(arg_keys[1], (2, R), 1.0, 6.0, (), jnp.float32),
        "filter_bank": centred(arg_keys[2], (2, CH, CH, M), CH ** -0.5, 2.0),
        "doppler_rate": jnp.clip(jnp.exp(math.log(400.0) - 2.9957323 * jax.random.uniform(arg_keys[3], (R,), jnp.float32) ** block_levels(arg_keys[3], (R,), ((0, 32),), -0.2, 0.2)), 20.0, 400.0),
        "doppler_width": plant(jax.random.randint(arg_keys[4], (R,), 2 * M, 4 * M + 1), jax.random.fold_in(arg_keys[4], 1), 2 * M, 4 * M).astype(jnp.int32),
        "migration": draw_migration(jax.random.fold_in(arg_keys[6], 71), 0),
    }


def dft_table(length, sense):
    positions = jnp.arange(length, dtype=jnp.int32)
    product = (positions[:, None] * positions[None, :]) % length
    angles = (2.0 * math.pi / length) * product.astype(jnp.float32)
    cosine = jnp.cos(angles)
    sine_part = sense * jnp.sin(angles)
    return jnp.stack([jnp.stack([cosine, -sine_part]), jnp.stack([sine_part, cosine])]).astype(jnp.bfloat16)


def phase_pair(product, length, sense):
    angles = (2.0 * math.pi / length) * (product % length).astype(jnp.float32)
    return jnp.cos(angles), sense * jnp.sin(angles)


def complex_scale(values, real_part, imag_part):
    return jnp.stack([values[0] * real_part - values[1] * imag_part, values[0] * imag_part + values[1] * real_part])


def contract(form, matrix, values):
    return jnp.einsum(form, matrix.astype(jnp.float32), values.astype(jnp.float32))


def range_compress(samples, replica):
    row_count = samples.shape[1]
    length = RA * RB
    blocks = samples.reshape(2, row_count, RB, RA)
    row_ids = jnp.arange(RB, dtype=jnp.int32)[:, None]
    col_ids = jnp.arange(RA, dtype=jnp.int32)[None, :]
    current = contract("oiub,inba->onua", dft_table(RB, -1.0), blocks)
    real_part, imag_part = phase_pair(row_ids * col_ids, length, -1.0)
    current = complex_scale(current, real_part, imag_part).astype(jnp.bfloat16)
    current = contract("oika,inua->onuk", dft_table(RA, -1.0), current)
    spectrum = replica.reshape(2, RA, RB).transpose(0, 2, 1)
    current = complex_scale(current, spectrum[0], spectrum[1]).astype(jnp.bfloat16)
    current = contract("oiak,inuk->onua", dft_table(RA, 1.0), current)
    real_part, imag_part = phase_pair(row_ids * col_ids, length, 1.0)
    current = complex_scale(current, real_part, imag_part).astype(jnp.bfloat16)
    current = contract("oibu,inua->onba", dft_table(RB, 1.0), current)
    return (current * (1.0 / length)).astype(jnp.bfloat16).reshape(2, row_count, length)


def azimuth_forward(extended):
    row_count = extended.shape[1]
    length = extended.shape[2]
    col_width = extended.shape[3]
    inner_len = length // MB
    blocks = extended.reshape(2, row_count, MB, inner_len, col_width)
    current = contract("oiub,icbaw->ocuaw", dft_table(MB, -1.0), blocks)
    freq_ids = jnp.arange(MB, dtype=jnp.int32)[:, None, None]
    pos_ids = jnp.arange(inner_len, dtype=jnp.int32)[None, :, None]
    real_part, imag_part = phase_pair(freq_ids * pos_ids, length, -1.0)
    current = complex_scale(current, real_part, imag_part).astype(jnp.bfloat16)
    return contract("oiva,icuaw->ocuvw", dft_table(inner_len, -1.0), current).astype(jnp.bfloat16)


def azimuth_finish(spectra, filter_bank, doppler_rate, doppler_width, migration, pulse_block):
    inner_len = spectra.shape[3]
    length = MB * inner_len
    out_width = doppler_rate.shape[0]
    bank = filter_bank.reshape(2, CH, CH, inner_len, MB).transpose(0, 1, 2, 4, 3)
    matrix = jnp.stack([jnp.stack([bank[0], -bank[1]]), jnp.stack([bank[1], bank[0]])])
    combined = contract("oijcuv,icuvw->ojuvw", matrix, spectra)
    subband = jnp.arange(CH, dtype=jnp.int32)[:, None, None]
    fine_ids = jnp.arange(MB, dtype=jnp.int32)[None, :, None]
    coarse_ids = jnp.arange(inner_len, dtype=jnp.int32)[None, None, :]
    spectrum_len = CH * length
    half_len = spectrum_len // 2
    positions = subband * length + fine_ids + MB * coarse_ids
    centered = jnp.where(positions >= half_len, positions - spectrum_len, positions)
    offsets = (migration[None, None, None, :] * ((centered * centered) // half_len)[..., None]) // half_len
    columns = jnp.arange(out_width, dtype=jnp.int32)[None, None, None, :] + offsets
    shifted = jnp.take_along_axis(combined, jnp.broadcast_to(columns, (2,) + columns.shape), axis=4)
    normal = centered.astype(jnp.float32) / spectrum_len
    phases = doppler_rate[None, None, None, :] * (normal * normal)[..., None]
    inside_band = jnp.abs(centered)[..., None] < doppler_width[None, None, None, :]
    real_part = jnp.where(inside_band, jnp.cos(phases), 0.0)
    imag_part = jnp.where(inside_band, jnp.sin(phases), 0.0)
    filtered = complex_scale(shifted, real_part, imag_part).astype(jnp.bfloat16)
    current = contract("oiqj,ijuvw->oquvw", dft_table(CH, 1.0), filtered)
    real_part, imag_part = phase_pair(subband * (fine_ids + MB * coarse_ids), spectrum_len, 1.0)
    current = complex_scale(current, real_part[..., None], imag_part[..., None]).astype(jnp.bfloat16)
    current = contract("oiav,iquvw->oquaw", dft_table(inner_len, 1.0), current)
    real_part, imag_part = phase_pair(jnp.arange(MB, dtype=jnp.int32)[:, None] * jnp.arange(inner_len, dtype=jnp.int32)[None, :], length, 1.0)
    current = complex_scale(current, real_part[..., None], imag_part[..., None]).astype(jnp.bfloat16)
    current = contract("oibu,iquaw->obaqw", dft_table(MB, 1.0), current)
    current = (current * (1.0 / spectrum_len)).reshape(2, length, CH, out_width)
    return current[:, E:E + pulse_block].reshape(2, CH * pulse_block, out_width).astype(jnp.bfloat16)


def reference(echoes, replica, filter_bank, doppler_rate, doppler_width, migration):
    compressed = lax.map(lambda samples: range_compress(samples, replica), jnp.swapaxes(echoes, 0, 1))
    compressed = jnp.swapaxes(compressed, 0, 1)
    pulse_block = PULSES // N_AZ
    length = pulse_block + 2 * E
    padded = jnp.pad(compressed, ((0, 0), (0, 0), (E, E), (0, OV)))
    group_cols = R // 8
    outputs = []
    for block_id in range(N_AZ):
        block_data = padded[:, :, block_id * pulse_block:block_id * pulse_block + length, :]

        def one_group(group_id):
            start = (group_id * group_cols).astype(jnp.int32)
            columns = lax.dynamic_slice_in_dim(block_data, start, group_cols + OV, 3)
            spectra = azimuth_forward(columns)
            return azimuth_finish(spectra, filter_bank,
                                  lax.dynamic_slice_in_dim(doppler_rate, start, group_cols, 0),
                                  lax.dynamic_slice_in_dim(doppler_width, start, group_cols, 0),
                                  lax.dynamic_slice_in_dim(migration, start, group_cols, 0), pulse_block)

        pieces = lax.map(one_group, jnp.arange(8, dtype=jnp.int32))
        outputs.append(pieces.transpose(1, 2, 0, 3).reshape(2, CH * pulse_block, R))
    return jnp.concatenate(outputs, axis=1)
```

```python
import functools
import math

import jax
import jax.numpy as jnp
import ml_dtypes
import numpy as np
from jax import lax
from jax.experimental import pallas as pl
from jax.experimental.pallas import tpu as pltpu
from jax.sharding import PartitionSpec as P

CH = 8
RA = 128
RB = 64
R = RA * RB
M = 256
E = 64
OV = 32
N_AZ = 4
N_RG = 32
GROUP = 16
BLOCKS = M // GROUP
PART = 9
UNITS = 2 * PART
CUTS = ((0, 4), (4, 9), (9, 13), (13, 18))
MESH = pl.DeviceIdType.MESH
F32 = jnp.float32
BF16 = jnp.bfloat16


def stored(table):
    return np.asarray(table, np.float32).astype(ml_dtypes.bfloat16)


def angle_pair(product, length):
    angles = 2.0 * math.pi / length * (np.asarray(product) % length)
    return np.cos(angles), np.sin(angles)


def real_rows(cosine, sine):
    return np.stack(
        [np.stack([cosine, -sine], axis=1), np.stack([sine, cosine], axis=1)]
    )


def range_tables():
    ids = np.arange(RB)
    cosine, sine = angle_pair(ids[:, None] * ids[None, :], RB)
    w1 = real_rows(cosine, -sine).reshape(2 * RB, 2 * RB)
    w4 = real_rows(cosine, sine).reshape(2 * RB, 2 * RB) / R
    ids = np.arange(RA)
    cosine, sine = angle_pair(ids[:, None] * ids[None, :], RA)
    v2 = real_rows(cosine, -sine).reshape(2 * RA, 2 * RA).T
    v3 = real_rows(cosine, sine).reshape(2 * RA, 2 * RA).T
    cosine, sine = angle_pair(np.arange(RB)[:, None] * np.arange(RA)[None, :], R)
    twiddle = np.stack([cosine, sine]).astype(np.float32)
    return stored(w1), stored(v2), stored(v3), stored(w4), twiddle


def azimuth_tables():
    freqs = np.arange(M)
    cosine, sine = angle_pair(freqs[:, None] * np.arange(M)[None, :], M)
    forward = real_rows(cosine, -sine)
    forward = forward.reshape(2, M, 2, M // 4, 4).transpose(0, 1, 3, 2, 4).reshape(2 * M, 2 * M)
    slots = np.arange(E, M - E)
    inverse = []
    for q in range(CH):
        cosine, sine = angle_pair((CH * slots[:, None] + q) * freqs[None, :], CH * M)
        inverse.append(real_rows(cosine, sine).reshape(M, 2 * M) / (CH * M))
    ids = np.arange(CH)
    cosine, sine = angle_pair(ids[:, None] * ids[None, :], CH)
    merge = real_rows(cosine, sine).transpose(1, 0, 2, 3)
    merge = merge.transpose(0, 1, 3, 2).reshape(2 * CH, 2 * CH)
    merge = np.kron(merge, np.eye(GROUP))
    spread = np.zeros((2, CH, CH, CH, 2, CH, 2, GROUP))
    for j in range(CH):
        for c in range(CH):
            spread[0, j, c, j, 0, c, 0] = 1.0
            spread[1, j, c, j, 0, c, 1] = -1.0
            spread[1, j, c, j, 1, c, 0] = 1.0
            spread[0, j, c, j, 1, c, 1] = 1.0
    spread = spread.reshape(2 * CH * CH, 2 * CH * 2 * CH * GROUP)
    return stored(forward), stored(np.stack(inverse)), stored(merge), stored(spread)


def dot(a, b):
    return jnp.dot(a, b, preferred_element_type=F32)


def compress_kernel(
    x_ref, w1_ref, v2_ref, v3_ref, w4_ref, twiddle_ref, replica_ref, out_ref, turn, rim
):
    lane_group = lax.broadcasted_iota(jnp.int32, (N_RG * 8, RA), 1) // OV

    def scaled(real, imag, table, sense):
        tr, ti = table[0], table[1] * sense
        return real * tr - imag * ti, real * ti + imag * tr

    @pl.loop(0, 2)
    def _(g):
        for inner in range(4):
            base = (4 * g + inner) * 4
            columns = [
                jnp.concatenate([x_ref[0, base + p], x_ref[1, base + p]], axis=0)
                for p in range(4)
            ]
            first = dot(w1_ref[...], jnp.concatenate(columns, axis=1))
            rows = []
            for p in range(4):
                part = first[:, p * RA : (p + 1) * RA]
                pair = scaled(part[:RB], part[RB:], twiddle_ref, -1.0)
                rows.append(jnp.concatenate(pair, axis=1).astype(BF16))
            second = dot(jnp.concatenate(rows, axis=0), v2_ref[...])
            rows = []
            for p in range(4):
                part = second[p * RB : (p + 1) * RB]
                pair = scaled(part[:, :RA], part[:, RA:], replica_ref, 1.0)
                rows.append(jnp.concatenate(pair, axis=1).astype(BF16))
            third = dot(jnp.concatenate(rows, axis=0), v3_ref[...])
            columns = []
            for p in range(4):
                part = third[p * RB : (p + 1) * RB]
                pair = scaled(part[:, :RA], part[:, RA:], twiddle_ref, 1.0)
                columns.append(jnp.concatenate(pair, axis=0).astype(BF16))
            last = dot(w4_ref[...], jnp.concatenate(columns, axis=1))
            for o in range(2):
                for p in range(4):
                    turn[pl.ds(o * 4 + p, RB, stride=8), :] = last[
                        o * RB : (o + 1) * RB, p * RA : (p + 1) * RA
                    ]
            turned = turn[...].reshape(N_RG, 2, 8, RA)
            unit = PART * g + 2 * inner
            out_ref[:, unit] = turned[:, 0].astype(BF16)
            out_ref[:, unit + 1] = turned[:, 1].astype(BF16)
            edge = turned[:, 0].reshape(N_RG * 8, RA)
            if inner:
                edge = pltpu.roll(edge, OV * inner, 1)
                edge = jnp.where(lane_group == inner, edge, rim[...])
            rim[...] = edge
        unit = PART * g + 8
        kept = rim[...].astype(BF16).reshape(N_RG, 8, RA)
        out_ref[0 : N_RG - 1, unit] = kept[1:]
        out_ref[N_RG - 1, unit] = jnp.zeros((8, RA), BF16)


def range_compress(echoes, replica):
    tables = range_tables()
    samples = echoes.reshape(2, CH * 4, RB, RA)
    spectrum = replica.reshape(2, RA, RB).transpose(0, 2, 1)
    return pl.pallas_call(
        compress_kernel,
        out_shape=jax.ShapeDtypeStruct((N_RG, UNITS, 8, RA), BF16),
        in_specs=[pl.BlockSpec(memory_space=pltpu.VMEM)] * 7,
        out_specs=pl.BlockSpec(memory_space=pltpu.VMEM),
        scratch_shapes=[pltpu.VMEM((8 * RB, RA), F32), pltpu.VMEM((N_RG * 8, RA), F32)],
        compiler_params=pltpu.CompilerParams(vmem_limit_bytes=32 * 2**20),
        cost_estimate=pl.CostEstimate(
            flops=2 * 400_000_000, bytes_accessed=2**22, transcendentals=0
        ),
        name="range_compress",
    )(samples, *[jnp.asarray(t) for t in tables], spectrum)


def turn_kernel(sent, zeros, held, far_send, far_recv, near_send, near_recv, own_sem, zero_sem):
    block = lax.axis_index("az")
    me = lax.axis_index("rg")
    x, z, core = me // 8, (me // 2) % 4, me % 2
    above, below = (block + 1) % N_AZ, (block + N_AZ - 1) % N_AZ

    def peer(step):
        px = (x + step // 8) % 4
        pz = (z + (step // 2) % 4) % 4
        return px * 8 + pz * 2 + (core + step) % 2

    barrier = pltpu.get_barrier_semaphore()

    @pl.loop(1, N_RG)
    def _(step):
        pl.semaphore_signal(barrier, inc=1, device_id=(block, peer(step)), device_id_type=MESH)

    for other in (above, below):
        pl.semaphore_signal(barrier, inc=1, device_id=(other, me), device_id_type=MESH)
    pl.semaphore_wait(barrier, N_RG + 1)

    own = []
    for n, (low, high) in enumerate(CUTS):
        units = pl.ds(low, high - low)

        @pl.loop(1, N_RG)
        def _(step):
            target = peer(step)
            pltpu.make_async_remote_copy(
                src_ref=sent.at[target, units],
                dst_ref=held.at[16 + me, units],
                send_sem=far_send.at[n],
                recv_sem=far_recv.at[n],
                device_id=(block, target),
                device_id_type=MESH,
            ).start()

        copy = pltpu.make_async_copy(sent.at[me, units], held.at[16 + me, units], own_sem.at[n])
        copy.start()
        own.append(copy)

    def fill(at, sem):
        return pltpu.make_async_copy(zeros, held.at[pl.ds(at, 16)], sem)

    @pl.when(block == 0)
    def _():
        fill(0, zero_sem).start()

    @pl.when(block == N_AZ - 1)
    def _():
        fill(48, zero_sem).start()

    def onward(n, low, high, up):
        units = pl.ds(low, high - low)
        return pltpu.make_async_remote_copy(
            src_ref=held.at[pl.ds(32 if up else 16, 16), units],
            dst_ref=held.at[pl.ds(0 if up else 48, 16), units],
            send_sem=near_send.at[int(up), n],
            recv_sem=near_recv.at[int(up), n],
            device_id=(above if up else below, me),
            device_id_type=MESH,
        )

    for n, (low, high) in enumerate(CUTS):
        units = pl.ds(low, high - low)
        whole = held.at[pl.ds(16, N_RG - 1), units]
        pltpu.make_async_copy(whole, whole, far_recv.at[n]).wait()
        own[n].wait()

        @pl.when(block < N_AZ - 1)
        def _():
            onward(n, low, high, True).start()

        @pl.when(block > 0)
        def _():
            onward(n, low, high, False).start()

    for n, (low, high) in enumerate(CUTS):
        units = pl.ds(low, high - low)
        whole = held.at[pl.ds(16, N_RG - 1), units]
        pltpu.make_async_copy(whole, whole, far_send.at[n]).wait()

        @pl.when(block < N_AZ - 1)
        def _():
            onward(n, low, high, True).wait_send()
            onward(n, low, high, False).wait_recv()

        @pl.when(block > 0)
        def _():
            onward(n, low, high, False).wait_send()
            onward(n, low, high, True).wait_recv()

    @pl.when(block == 0)
    def _():
        fill(0, zero_sem).wait()

    @pl.when(block == N_AZ - 1)
    def _():
        fill(48, zero_sem).wait()


def corner_turn(sent):
    count = len(CUTS)
    return pl.pallas_call(
        turn_kernel,
        out_shape=jax.ShapeDtypeStruct((2 * N_RG, UNITS, 8, RA), BF16),
        in_specs=[pl.BlockSpec(memory_space=pl.ANY)] * 2,
        out_specs=pl.BlockSpec(memory_space=pl.ANY),
        scratch_shapes=[
            pltpu.SemaphoreType.DMA((count,)),
            pltpu.SemaphoreType.DMA((count,)),
            pltpu.SemaphoreType.DMA((2, count)),
            pltpu.SemaphoreType.DMA((2, count)),
            pltpu.SemaphoreType.DMA((count,)),
            pltpu.SemaphoreType.DMA,
        ],
        compiler_params=pltpu.CompilerParams(collective_id=0, has_side_effects=True),
        cost_estimate=pl.CostEstimate(flops=0, bytes_accessed=2**22, transcendentals=0),
        name="corner_turn",
    )(sent, jnp.zeros((16, UNITS, 8, RA), BF16))


def sine_cosine(angle):
    turns = angle * (2.0 / math.pi)
    quarter = (turns + 0.5).astype(jnp.int32)
    rest = (turns - quarter.astype(F32)) * (0.5 * math.pi)
    square = rest * rest
    sine = -1.9515295891e-4 * square + 8.3321608736e-3
    sine = sine * square - 1.6666654611e-1
    sine = sine * square * rest + rest
    cosine = 2.443315711809948e-5 * square - 1.388731625493765e-3
    cosine = cosine * square + 4.166664568298827e-2
    cosine = cosine * square * square - 0.5 * square + 1.0
    swap = quarter % 2 == 1
    real = jnp.where(swap, sine, cosine)
    imag = jnp.where(swap, cosine, sine)
    real = jnp.where((quarter + 1) % 4 >= 2, -real, real)
    imag = jnp.where(quarter % 4 >= 2, -imag, imag)
    return real, imag


def finish_kernel(
    held,
    bank_ref,
    rate_ref,
    width_ref,
    migration_ref,
    forward_ref,
    inverse_ref,
    merge_ref,
    spread_ref,
    out_ref,
    matrix,
    doppler,
    merged,
    left,
    right,
):
    same = (
        lax.broadcasted_iota(jnp.int32, (M, M), 0) % GROUP
        == lax.broadcasted_iota(jnp.int32, (M, M), 1) % GROUP
    )
    for n in range(2 * CH):
        wide = lax.dot_general(
            bank_ref[...],
            spread_ref[:, n * M : (n + 1) * M],
            (((0,), (0,)), ((), ())),
            preferred_element_type=F32,
        )
        wide = jnp.where(same, wide, 0.0).astype(BF16)
        matrix[:, n * GROUP : (n + 1) * GROUP, :] = wide.reshape(BLOCKS, GROUP, M)

    def gathered(unit):
        return held[:, unit].astype(F32).reshape(2 * M, RA).astype(BF16)

    @pl.loop(0, 2)
    def _(g):
        for inner in range(4):
            unit = PART * g + 2 * inner
            pulses = jnp.concatenate([gathered(unit), gathered(unit + 1)], axis=1)
            bins = dot(forward_ref[...], pulses).astype(BF16)
            for o in range(2):
                doppler[:, 2 * (4 * g + inner) + o, :, 0 : 2 * RA] = bins[
                    o * M : (o + 1) * M
                ].reshape(BLOCKS, GROUP, 2 * RA)
        bins = dot(forward_ref[...], gathered(PART * g + 8))
        for inner in range(4):
            turned = pltpu.roll(bins, RA - OV * inner, 1) if inner else bins
            turned = turned.astype(BF16)
            for o in range(2):
                doppler[:, 2 * (4 * g + inner) + o, :, 2 * RA : 3 * RA] = turned[
                    o * M : (o + 1) * M
                ].reshape(BLOCKS, GROUP, RA)

    shape = (GROUP, RA)
    lane = lax.broadcasted_iota(jnp.int32, shape, 1)
    row = lax.broadcasted_iota(jnp.int32, shape, 0)

    @pl.loop(0, BLOCKS)
    def _(g):
        bands = dot(matrix[g], doppler[g].reshape(M, 3 * RA))
        rows = []
        for j in range(CH):
            centered = row + (g * GROUP + (j * M if j < CH // 2 else j * M - CH * M))
            level = (centered * centered) // (CH * M // 2)
            normal = centered.astype(F32) * (1.0 / (CH * M))
            normal = normal * normal
            real_band = bands[2 * j * GROUP : (2 * j + 1) * GROUP]
            imag_band = bands[(2 * j + 1) * GROUP : (2 * j + 2) * GROUP]
            real_parts, imag_parts = [], []
            for h in range(2):
                cols = slice(h * RA, (h + 1) * RA)
                after = slice((h + 1) * RA, (h + 2) * RA)
                offsets = (migration_ref[:, cols] * level) // (CH * M // 2)
                place = lane + offsets
                here = place < RA
                place = place % RA

                def pick(band):
                    near = jnp.take_along_axis(band[:, cols], place, axis=1)
                    far = jnp.take_along_axis(band[:, after], place, axis=1)
                    return jnp.where(here, near, far)

                real, imag = pick(real_band), pick(imag_band)
                phase_real, phase_imag = sine_cosine(rate_ref[:, cols] * normal)
                inside = jnp.abs(centered) < width_ref[:, cols]
                phase_real = jnp.where(inside, phase_real, 0.0)
                phase_imag = jnp.where(inside, phase_imag, 0.0)
                real_parts.append(real * phase_real - imag * phase_imag)
                imag_parts.append(real * phase_imag + imag * phase_real)
            rows.append(jnp.concatenate(real_parts, axis=1).astype(BF16))
            rows.append(jnp.concatenate(imag_parts, axis=1).astype(BF16))
        mixed = dot(merge_ref[...], jnp.concatenate(rows, axis=0)).astype(BF16)
        merged[:, :, g] = mixed.reshape(CH, 2, GROUP, 2 * RA)

    @pl.loop(0, CH)
    def _(q):
        image = dot(inverse_ref[q], merged[q].reshape(2 * M, 2 * RA))
        for o in range(2):
            part = image[o * RA : (o + 1) * RA]
            where = pl.ds(o * CH * RA + q, RA, stride=CH)
            left[where, :] = part[:, :RA]
            right[where, :] = part[:, RA:]

    for o in range(2):
        where = slice(o * CH * RA, (o + 1) * CH * RA)
        out_ref[o, :, :RA] = left[where, :].astype(BF16)
        out_ref[o, :, RA:] = right[where, :].astype(BF16)


def azimuth_finish(held, filter_bank, doppler_rate, doppler_width, migration):
    tables = azimuth_tables()
    vmem = pl.BlockSpec(memory_space=pltpu.VMEM)
    return pl.pallas_call(
        finish_kernel,
        out_shape=jax.ShapeDtypeStruct((2, CH * RA, 2 * RA), BF16),
        in_specs=[vmem] * 9,
        out_specs=vmem,
        scratch_shapes=[
            pltpu.VMEM((BLOCKS, M, M), BF16),
            pltpu.VMEM((BLOCKS, 2 * CH, GROUP, 3 * RA), BF16),
            pltpu.VMEM((CH, 2, BLOCKS, GROUP, 2 * RA), BF16),
            pltpu.VMEM((2 * CH * RA, RA), F32),
            pltpu.VMEM((2 * CH * RA, RA), F32),
        ],
        compiler_params=pltpu.CompilerParams(vmem_limit_bytes=48 * 2**20),
        cost_estimate=pl.CostEstimate(
            flops=2 * 1_600_000_000, bytes_accessed=2**23, transcendentals=0
        ),
        name="azimuth_finish",
    )(
        held,
        filter_bank.reshape(2 * CH * CH, M),
        doppler_rate.reshape(1, 2 * RA),
        doppler_width.reshape(1, 2 * RA),
        migration.reshape(1, 2 * RA),
        *[jnp.asarray(t) for t in tables],
    )


def shards(echoes, replica, filter_bank, doppler_rate, doppler_width, migration):
    held = corner_turn(range_compress(echoes, replica))
    return azimuth_finish(held, filter_bank, doppler_rate, doppler_width, migration)


def solution(mesh):
    placed = (P(None, None, ("az", "rg"), None), P(), P(), P("rg"), P("rg"), P("rg"))
    return jax.shard_map(
        shards, mesh=mesh, in_specs=placed, out_specs=P(None, "az", "rg"), check_vma=False
    )
```

```python
import functools
import math

import jax
import jax.numpy as jnp
import ml_dtypes
import numpy as np
from jax import lax
from jax.experimental import pallas as pl
from jax.experimental.pallas import tpu as pltpu
from jax.sharding import PartitionSpec as P

CH = 8
RA = 128
RB = 64
R = RA * RB
M = 256
E = 64
OV = 32
N_AZ = 4
N_RG = 32
GROUP = 16
BLOCKS = M // GROUP
UNITS = 18
CUTS = ((0, 2), (2, 5), (5, 10), (10, 14), (14, 18))
MESH = pl.DeviceIdType.MESH
F32 = jnp.float32
BF16 = jnp.bfloat16


def stored(table):
    return np.asarray(table, np.float32).astype(ml_dtypes.bfloat16)


def angle_pair(product, length):
    angles = 2.0 * math.pi / length * (np.asarray(product) % length)
    return np.cos(angles), np.sin(angles)


def real_rows(cosine, sine):
    return np.stack(
        [np.stack([cosine, -sine], axis=1), np.stack([sine, cosine], axis=1)]
    )


def unit_of(channel, half):
    return channel + channel // 4 if half else 10 + channel


def edge_unit(group):
    return 5 * group + 4


def range_tables():
    ids = np.arange(RB)
    cosine, sine = angle_pair(ids[:, None] * ids[None, :], RB)
    w1 = real_rows(cosine, -sine).reshape(2 * RB, 2 * RB)
    w4 = real_rows(cosine, sine) / R
    w4 = np.einsum("obik,pn->bopink", w4, np.eye(4)).reshape(8 * RB, 8 * RB)
    ids = np.arange(RA)
    order = 2 * (ids % RB) + ids // RB
    cosine, sine = angle_pair(ids[:, None] * ids[None, :], RA)
    v2 = real_rows(cosine, -sine)[:, order].reshape(2 * RA, 2 * RA).T
    v3 = real_rows(cosine, sine)[..., order].reshape(2 * RA, 2 * RA).T
    cosine, sine = angle_pair(np.arange(RB)[:, None] * np.arange(RA)[None, :], R)
    twiddle = np.stack([cosine, sine]).astype(np.float32)
    return stored(w1), stored(v2), stored(v3), stored(w4), twiddle


def azimuth_tables():
    freqs = np.arange(M)
    cosine, sine = angle_pair(freqs[:, None] * np.arange(M)[None, :], M)
    forward = real_rows(cosine, -sine)
    forward = forward.reshape(2, M, 2, M // 4, 4).transpose(0, 1, 3, 2, 4).reshape(2 * M, 2 * M)
    slots = np.arange(E, M - E)
    inverse = []
    for q in range(CH):
        cosine, sine = angle_pair((CH * slots[:, None] + q) * freqs[None, :], CH * M)
        inverse.append(real_rows(cosine, sine).reshape(M, 2 * M) / (CH * M))
    ids = np.arange(CH)
    cosine, sine = angle_pair(ids[:, None] * ids[None, :], CH)
    merge = real_rows(cosine, sine).transpose(1, 0, 2, 3)
    merge = merge.transpose(0, 1, 3, 2).reshape(2 * CH, 2 * CH)
    merge = np.kron(merge, np.eye(GROUP))
    spread = np.zeros((2, CH, CH, CH, 2, CH, 2, GROUP))
    for j in range(CH):
        for c in range(CH):
            spread[0, j, c, j, 0, c, 0] = 1.0
            spread[1, j, c, j, 0, c, 1] = -1.0
            spread[1, j, c, j, 1, c, 0] = 1.0
            spread[0, j, c, j, 1, c, 1] = 1.0
    spread = spread.reshape(2 * CH * CH, 2 * CH * 2 * CH * GROUP)
    return stored(forward), stored(np.stack(inverse)), stored(merge), stored(spread)


def dot(a, b):
    return jnp.dot(a, b, preferred_element_type=F32)


def scaled(real, imag, table_real, table_imag):
    return (
        real * table_real - imag * table_imag,
        real * table_imag + imag * table_real,
    )


def load_spectrum(replica, natural, spectrum):
    values = replica[...]
    for n in range(RB):
        natural[pl.ds(n, 2, stride=RB), :] = values[:, n * RA : (n + 1) * RA]
    turned = natural[...].T
    for i in range(2):
        part = turned[:, i * RB : (i + 1) * RB]
        spectrum[i] = jnp.concatenate([part[:RB], part[RB:]], axis=1)


def compress_pair(first_channel, inner, x, tables, spectrum, turn, rim, sent):
    w1, v2, v3, w4, twiddle = tables
    results = []
    for c in range(2):
        channel = first_channel + c
        for i in range(2):
            values = x[i, channel].astype(F32)
            for n in range(RB):
                turn[c, i, pl.ds(n, 4, stride=RB), :] = values[:, n * RA : (n + 1) * RA]
        columns = [
            jnp.concatenate(
                [turn[c, i, p * RB : (p + 1) * RB, :] for i in range(2)], axis=0
            ).astype(BF16)
            for p in range(4)
        ]
        current = dot(w1[...], jnp.concatenate(columns, axis=1))
        rows = []
        for p in range(4):
            part = current[:, p * RA : (p + 1) * RA]
            pair = scaled(part[:RB], part[RB:], twiddle[0], -twiddle[1])
            rows.append(jnp.concatenate(pair, axis=1).astype(BF16))
        current = dot(jnp.concatenate(rows, axis=0), v2[...])
        rows = []
        for p in range(4):
            part = current[p * RB : (p + 1) * RB]
            pair = scaled(part[:, :RA], part[:, RA:], spectrum[0], spectrum[1])
            rows.append(jnp.concatenate(pair, axis=1).astype(BF16))
        current = dot(jnp.concatenate(rows, axis=0), v3[...])
        parts = []
        for p in range(4):
            part = current[p * RB : (p + 1) * RB]
            parts.append(scaled(part[:, :RA], part[:, RA:], twiddle[0], twiddle[1]))
        results.append(
            jnp.concatenate([parts[p][i] for i in range(2) for p in range(4)], axis=0).astype(BF16)
        )
    current = dot(w4[...], jnp.concatenate(results, axis=1))
    lane_group = lax.broadcasted_iota(jnp.int32, (N_RG * 8, RA), 1) // OV
    edge = rim[...] if inner else None
    for c in range(2):
        turned = current[:, c * RA : (c + 1) * RA].reshape(N_RG, 2, 8, RA)
        for half in range(2):
            sent[:, unit_of(first_channel + c, half)] = turned[:, half].astype(BF16)
        low = turned[:, 0].reshape(N_RG * 8, RA)
        spot = 2 * inner + c
        if spot:
            edge = jnp.where(lane_group == spot, pltpu.roll(low, OV * spot, 1), edge)
        else:
            edge = low
    if not inner:
        rim[...] = edge
        return
    unit = edge_unit(first_channel // 4)
    kept = edge.astype(BF16).reshape(N_RG, 8, RA)
    sent[0 : N_RG - 1, unit] = kept[1:]
    sent[N_RG - 1, unit] = jnp.zeros((8, RA), BF16)


def sine_cosine(angle):
    turns = angle * (2.0 / math.pi)
    quarter = (turns + 0.5).astype(jnp.int32)
    rest = (turns - quarter.astype(F32)) * (0.5 * math.pi)
    square = rest * rest
    sine = -1.9515295891e-4 * square + 8.3321608736e-3
    sine = sine * square - 1.6666654611e-1
    sine = sine * square * rest + rest
    cosine = 2.443315711809948e-5 * square - 1.388731625493765e-3
    cosine = cosine * square + 4.166664568298827e-2
    cosine = cosine * square * square - 0.5 * square + 1.0
    swap = quarter % 2 == 1
    real = jnp.where(swap, sine, cosine)
    imag = jnp.where(swap, cosine, sine)
    real = jnp.where((quarter + 1) % 4 >= 2, -real, real)
    imag = jnp.where(quarter % 4 >= 2, -imag, imag)
    return real, imag


def build_matrix(bank, spread, matrix):
    same = (
        lax.broadcasted_iota(jnp.int32, (M, M), 0) % GROUP
        == lax.broadcasted_iota(jnp.int32, (M, M), 1) % GROUP
    )
    for n in range(2 * CH):
        wide = lax.dot_general(
            bank[...],
            spread[:, n * M : (n + 1) * M],
            (((0,), (0,)), ((), ())),
            preferred_element_type=F32,
        )
        wide = jnp.where(same, wide, 0.0).astype(BF16)
        matrix[:, n * GROUP : (n + 1) * GROUP, :] = wide.reshape(BLOCKS, GROUP, M)


def build_phases(g, half, rate, width, migration, phase, place):
    cols = slice(half * RA, (half + 1) * RA)
    row = lax.broadcasted_iota(jnp.int32, (GROUP, RA), 0)
    lane = lax.broadcasted_iota(jnp.int32, (GROUP, RA), 1)
    for j in range(CH):
        centered = row + (g * GROUP + (j * M if j < CH // 2 else j * M - CH * M))
        level = (centered * centered) // (CH * M // 2)
        normal = centered.astype(F32) * (1.0 / (CH * M))
        offsets = (migration[:, cols] * level) // (CH * M // 2)
        place[half, g, j] = lane + offsets
        real, imag = sine_cosine(rate[:, cols] * (normal * normal))
        inside = jnp.abs(centered) < width[:, cols]
        phase[half, g, 2 * j] = jnp.where(inside, real, 0.0)
        phase[half, g, 2 * j + 1] = jnp.where(inside, imag, 0.0)


def gathered(held, unit):
    return held[:, unit].astype(F32).reshape(2 * M, RA).astype(BF16)


def forward_pair(channel, half, held, forward, doppler):
    units = [unit_of(channel + n, half) for n in range(2)]
    pulses = jnp.concatenate([gathered(held, unit) for unit in units], axis=1)
    bins = dot(forward[...], pulses).astype(BF16)
    for n in range(2):
        for o in range(2):
            doppler[half, :, 2 * (channel + n) + o] = bins[
                o * M : (o + 1) * M, n * RA : (n + 1) * RA
            ].reshape(BLOCKS, GROUP, RA)


def forward_edges(held, forward, doppler):
    pulses = jnp.concatenate([gathered(held, edge_unit(n)) for n in range(2)], axis=1)
    bins = dot(forward[...], pulses)
    for channel in range(CH):
        group, inner = channel // 4, channel % 4
        part = bins[:, group * RA : (group + 1) * RA]
        if inner:
            part = pltpu.roll(part, RA - OV * inner, 1)
        part = part.astype(BF16)
        for o in range(2):
            doppler[2, :, 2 * channel + o] = part[o * M : (o + 1) * M].reshape(BLOCKS, GROUP, RA)


def correct(g, half, matrix, doppler, bands, phase, place, merge, merged):
    low = doppler[half, g].reshape(M, RA)
    if half:
        both = dot(matrix[g], jnp.concatenate([low, doppler[2, g].reshape(M, RA)], axis=1))
        near, far = both[:, :RA], both[:, RA:]
        bands[g] = near
    else:
        near, far = dot(matrix[g], low), bands[g]
    rows = []
    for j in range(CH):
        spot = place[half, g, j]
        here = spot < RA
        spot = spot % RA

        def pick(part):
            at = slice(part * GROUP, (part + 1) * GROUP)
            return jnp.where(
                here,
                jnp.take_along_axis(near[at], spot, axis=1),
                jnp.take_along_axis(far[at], spot, axis=1),
            )

        real, imag = scaled(
            pick(2 * j), pick(2 * j + 1), phase[half, g, 2 * j], phase[half, g, 2 * j + 1]
        )
        rows += [real.astype(BF16), imag.astype(BF16)]
    mixed = dot(merge[...], jnp.concatenate(rows, axis=0)).astype(BF16)
    merged[:, :, g] = mixed.reshape(CH, 2, GROUP, RA)


def invert(q, inverse, merged, image):
    part = dot(inverse[q], merged[q].reshape(2 * M, RA))
    for o in range(2):
        image[pl.ds(o * CH * RA + q, RA, stride=CH), :] = part[o * RA : (o + 1) * RA]


def focus_kernel(
    x_hbm,
    replica,
    bank,
    rate,
    width,
    migration,
    w1,
    v2,
    v3,
    w4_hbm,
    twiddle,
    forward_hbm,
    inverse_hbm,
    merge,
    spread_hbm,
    out_hbm,
    x,
    w4,
    forward,
    inverse,
    spread,
    natural,
    spectrum,
    turn,
    rim,
    sent,
    held,
    matrix,
    doppler,
    bands,
    phase,
    place,
    merged,
    image,
    result,
    x_sem,
    table_sem,
    far_send,
    far_recv,
    near_send,
    near_recv,
    own_sem,
    out_sem,
):
    block = lax.axis_index("az")
    me = lax.axis_index("rg")
    px, pz, core = me // 8, (me // 2) % 4, me % 2
    above, below = (block + 1) % N_AZ, (block + N_AZ - 1) % N_AZ

    def peer(step):
        to_x = (px + step // 8) % 4
        to_z = (pz + (step // 2) % 4) % 4
        return to_x * 8 + to_z * 2 + (core + step) % 2

    fetches = [
        pltpu.make_async_copy(x_hbm.at[:, pl.ds(2 * n, 2)], x.at[:, pl.ds(2 * n, 2)], x_sem.at[n])
        for n in range(4)
    ]
    tables = [
        pltpu.make_async_copy(source, target, table_sem.at[n])
        for n, (source, target) in enumerate(
            [(w4_hbm, w4), (forward_hbm, forward), (spread_hbm, spread), (inverse_hbm, inverse)]
        )
    ]
    for copy in fetches + tables:
        copy.start()

    barrier = pltpu.get_barrier_semaphore()

    @pl.loop(1, N_RG)
    def _(step):
        pl.semaphore_signal(barrier, inc=1, device_id=(block, peer(step)), device_id_type=MESH)

    for other in (above, below):
        pl.semaphore_signal(barrier, inc=1, device_id=(other, me), device_id_type=MESH)

    own = [
        pltpu.make_async_copy(
            sent.at[me, pl.ds(low, high - low)],
            held.at[16 + me, pl.ds(low, high - low)],
            own_sem.at[n],
        )
        for n, (low, high) in enumerate(CUTS)
    ]

    def send(n):
        low, high = CUTS[n]
        units = pl.ds(low, high - low)

        @pl.loop(1, N_RG)
        def _(step):
            target = peer(step)
            pltpu.make_async_remote_copy(
                src_ref=sent.at[target, units],
                dst_ref=held.at[16 + me, units],
                send_sem=far_send.at[n],
                recv_sem=far_recv.at[n],
                device_id=(block, target),
                device_id_type=MESH,
            ).start()

        own[n].start()

    def onward(n, up):
        low, high = CUTS[n]
        units = pl.ds(low, high - low)
        return pltpu.make_async_remote_copy(
            src_ref=held.at[pl.ds(32 if up else 16, 16), units],
            dst_ref=held.at[pl.ds(0 if up else 48, 16), units],
            send_sem=near_send.at[int(up), n],
            recv_sem=near_recv.at[int(up), n],
            device_id=(above if up else below, me),
            device_id_type=MESH,
        )

    def relay(n):
        low, high = CUTS[n]
        whole = held.at[pl.ds(16, N_RG - 1), pl.ds(low, high - low)]
        pltpu.make_async_copy(whole, whole, far_recv.at[n]).wait()
        own[n].wait()

        @pl.when(block < N_AZ - 1)
        def _():
            onward(n, True).start()

        @pl.when(block > 0)
        def _():
            onward(n, False).start()

    def arrive(n):
        @pl.when(block < N_AZ - 1)
        def _():
            onward(n, False).wait_recv()

        @pl.when(block > 0)
        def _():
            onward(n, True).wait_recv()

    load_spectrum(replica, natural, spectrum)
    small = (w1, v2, v3, w4, twiddle)
    for n in range(4):
        fetches[n].wait()
        if n == 0:
            tables[0].wait()
        compress_pair(2 * n, n % 2, x, small, spectrum, turn, rim, sent)
        if n == 0:
            pl.semaphore_wait(barrier, N_RG + 1)
        if n < 2:
            send(n)
        if n == 3:
            for chunk in range(2, len(CUTS)):
                send(chunk)

    @pl.when(block == 0)
    def _():
        held[0:16] = jnp.zeros((16, UNITS, 8, RA), BF16)

    @pl.when(block == N_AZ - 1)
    def _():
        held[48:64] = jnp.zeros((16, UNITS, 8, RA), BF16)

    def phases(half, low, high):
        @pl.loop(low, high)
        def _(g):
            build_phases(g, half, rate, width, migration, phase, place)

    relay(0)
    tables[2].wait()
    build_matrix(bank, spread, matrix)
    phases(1, 0, 4)
    relay(1)
    phases(1, 4, 16)
    relay(2)
    phases(0, 0, 8)
    tables[1].wait()
    tables[3].wait()
    relay(3)
    phases(0, 8, 16)
    arrive(0)
    arrive(1)
    forward_pair(0, 1, held, forward, doppler)
    forward_pair(2, 1, held, forward, doppler)
    relay(4)
    arrive(2)
    forward_pair(4, 1, held, forward, doppler)
    forward_pair(6, 1, held, forward, doppler)
    forward_edges(held, forward, doppler)

    writes = [
        pltpu.make_async_copy(
            result.at[half], out_hbm.at[:, :, pl.ds(half * RA, RA)], out_sem.at[half]
        )
        for half in range(2)
    ]

    def complete(half):
        for g in range(BLOCKS):
            correct(g, half, matrix, doppler, bands, phase, place, merge, merged)
        for q in range(CH):
            invert(q, inverse, merged, image)

        result[half] = image[...].astype(BF16).reshape(2, CH * RA, RA)
        writes[half].start()

    complete(1)
    arrive(3)
    forward_pair(0, 0, held, forward, doppler)
    forward_pair(2, 0, held, forward, doppler)
    arrive(4)
    forward_pair(4, 0, held, forward, doppler)
    forward_pair(6, 0, held, forward, doppler)
    complete(0)

    for n, (low, high) in enumerate(CUTS):
        whole = held.at[pl.ds(16, N_RG - 1), pl.ds(low, high - low)]
        pltpu.make_async_copy(whole, whole, far_send.at[n]).wait()

        @pl.when(block < N_AZ - 1)
        def _():
            onward(n, True).wait_send()

        @pl.when(block > 0)
        def _():
            onward(n, False).wait_send()

    for copy in writes:
        copy.wait()


def shards(echoes, replica, filter_bank, doppler_rate, doppler_width, migration):
    w1, v2, v3, w4, twiddle = range_tables()
    forward, inverse, merge, spread = azimuth_tables()
    vmem = pl.BlockSpec(memory_space=pltpu.VMEM)
    hbm = pl.BlockSpec(memory_space=pl.ANY)
    count = len(CUTS)
    return pl.pallas_call(
        focus_kernel,
        out_shape=jax.ShapeDtypeStruct((2, CH * RA, 2 * RA), BF16),
        in_specs=[hbm] + [vmem] * 8 + [hbm, vmem, hbm, hbm, vmem, hbm],
        out_specs=hbm,
        scratch_shapes=[
            pltpu.VMEM((2, CH, 4, R), BF16),
            pltpu.VMEM((8 * RB, 8 * RB), BF16),
            pltpu.VMEM((2 * M, 2 * M), BF16),
            pltpu.VMEM((CH, M, 2 * M), BF16),
            pltpu.VMEM((2 * CH * CH, 2 * CH * M), BF16),
            pltpu.VMEM((2 * RB, RA), F32),
            pltpu.VMEM((2, RB, RA), F32),
            pltpu.VMEM((2, 2, 4 * RB, RA), F32),
            pltpu.VMEM((N_RG * 8, RA), F32),
            pltpu.VMEM((N_RG, UNITS, 8, RA), BF16),
            pltpu.VMEM((2 * N_RG, UNITS, 8, RA), BF16),
            pltpu.VMEM((BLOCKS, M, M), BF16),
            pltpu.VMEM((3, BLOCKS, 2 * CH, GROUP, RA), BF16),
            pltpu.VMEM((BLOCKS, M, RA), F32),
            pltpu.VMEM((2, BLOCKS, 2 * CH, GROUP, RA), F32),
            pltpu.VMEM((2, BLOCKS, CH, GROUP, RA), jnp.int32),
            pltpu.VMEM((CH, 2, BLOCKS, GROUP, RA), BF16),
            pltpu.VMEM((2 * CH * RA, RA), F32),
            pltpu.VMEM((2, 2, CH * RA, RA), BF16),
            pltpu.SemaphoreType.DMA((4,)),
            pltpu.SemaphoreType.DMA((4,)),
            pltpu.SemaphoreType.DMA((count,)),
            pltpu.SemaphoreType.DMA((count,)),
            pltpu.SemaphoreType.DMA((2, count)),
            pltpu.SemaphoreType.DMA((2, count)),
            pltpu.SemaphoreType.DMA((count,)),
            pltpu.SemaphoreType.DMA((2,)),
        ],
        compiler_params=pltpu.CompilerParams(
            collective_id=0, has_side_effects=True, vmem_limit_bytes=48 * 2**20
        ),
        cost_estimate=pl.CostEstimate(
            flops=2 * 2_000_000_000, bytes_accessed=2**23, transcendentals=0
        ),
        name="focus",
    )(
        echoes,
        replica,
        filter_bank.reshape(2 * CH * CH, M),
        doppler_rate.reshape(1, 2 * RA),
        doppler_width.reshape(1, 2 * RA),
        migration.reshape(1, 2 * RA),
        *[jnp.asarray(t) for t in (w1, v2, v3, w4, twiddle, forward, inverse, merge, spread)],
    )


def solution(mesh):
    placed = (P(None, None, ("az", "rg"), None), P(), P(), P("rg"), P("rg"), P("rg"))
    return jax.shard_map(
        shards, mesh=mesh, in_specs=placed, out_specs=P(None, "az", "rg"), check_vma=False
    )
```

```python
import functools
import math

import jax
import jax.numpy as jnp
import ml_dtypes
import numpy as np
from jax import lax
from jax.experimental import pallas as pl
from jax.experimental.pallas import tpu as pltpu
from jax.sharding import PartitionSpec as P

CH = 8
RA = 128
RB = 64
R = RA * RB
M = 256
E = 64
OV = 32
N_AZ = 4
N_RG = 32
GROUP = 16
BLOCKS = M // GROUP
UNITS = 18
CUTS = tuple((n, n + 2) for n in range(0, UNITS, 2))
FAR_FIRST = ((2, 2), (1, 2), (2, 1), (3, 2), (2, 3), (1, 1), (3, 3), (1, 3), (3, 1))
FAR_FIRST += ((2, 0), (0, 2), (1, 0), (0, 1), (3, 0), (0, 3), (0, 0))
MESH = pl.DeviceIdType.MESH
F32 = jnp.float32
BF16 = jnp.bfloat16


def stored(table):
    return np.asarray(table, np.float32).astype(ml_dtypes.bfloat16)


def angle_pair(product, length):
    angles = 2.0 * math.pi / length * (np.asarray(product) % length)
    return np.cos(angles), np.sin(angles)


def real_rows(cosine, sine):
    return np.stack(
        [np.stack([cosine, -sine], axis=1), np.stack([sine, cosine], axis=1)]
    )


def unit_of(channel, half):
    return channel if half else 10 + channel


def edge_unit(group):
    return CH + group


def range_tables():
    ids = np.arange(RB)
    cosine, sine = angle_pair(ids[:, None] * ids[None, :], RB)
    w1 = real_rows(cosine, -sine).reshape(2 * RB, 2 * RB)
    w4 = real_rows(cosine, sine) / R
    w4 = np.einsum("obik,pn->bopink", w4, np.eye(4)).reshape(8 * RB, 8 * RB)
    ids = np.arange(RA)
    order = 2 * (ids % RB) + ids // RB
    cosine, sine = angle_pair(ids[:, None] * ids[None, :], RA)
    v2 = real_rows(cosine, -sine)[:, order].reshape(2 * RA, 2 * RA).T
    v3 = real_rows(cosine, sine)[..., order].reshape(2 * RA, 2 * RA).T
    cosine, sine = angle_pair(np.arange(RB)[:, None] * np.arange(RA)[None, :], R)
    twiddle = np.stack([cosine, sine]).astype(np.float32)
    return stored(w1), stored(v2), stored(v3), stored(w4), twiddle


def azimuth_tables():
    freqs = np.arange(M)
    cosine, sine = angle_pair(freqs[:, None] * np.arange(M)[None, :], M)
    forward = real_rows(cosine, -sine)
    forward = forward.reshape(2, M, 2, M // 4, 4).transpose(0, 1, 3, 2, 4).reshape(2 * M, 2 * M)
    slots = np.arange(E, M - E)
    inverse = []
    for q in range(CH):
        cosine, sine = angle_pair((CH * slots[:, None] + q) * freqs[None, :], CH * M)
        inverse.append(real_rows(cosine, sine).reshape(M, 2 * M) / (CH * M))
    ids = np.arange(CH)
    cosine, sine = angle_pair(ids[:, None] * ids[None, :], CH)
    merge = real_rows(cosine, sine).transpose(1, 0, 2, 3)
    merge = merge.transpose(0, 1, 3, 2).reshape(2 * CH, 2 * CH)
    merge = np.kron(merge, np.eye(GROUP))
    spread = np.zeros((2, CH, CH, CH, 2, CH, 2, GROUP))
    for j in range(CH):
        for c in range(CH):
            spread[0, j, c, j, 0, c, 0] = 1.0
            spread[1, j, c, j, 0, c, 1] = -1.0
            spread[1, j, c, j, 1, c, 0] = 1.0
            spread[0, j, c, j, 1, c, 1] = 1.0
    spread = spread.reshape(2 * CH * CH, 2 * CH * 2 * CH * GROUP)
    return stored(forward), stored(np.stack(inverse)), stored(merge), stored(spread)


def dot(a, b):
    return jnp.dot(a, b, preferred_element_type=F32)


def scaled(real, imag, table_real, table_imag):
    return (
        real * table_real - imag * table_imag,
        real * table_imag + imag * table_real,
    )


def load_spectrum(replica, natural, spectrum):
    values = replica[...]
    for n in range(RB):
        natural[pl.ds(n, 2, stride=RB), :] = values[:, n * RA : (n + 1) * RA]
    turned = natural[...].T
    for i in range(2):
        part = turned[:, i * RB : (i + 1) * RB]
        spectrum[i] = jnp.concatenate([part[:RB], part[RB:]], axis=1)


def compress_pair(first_channel, inner, x, tables, spectrum, turn, rim, sent):
    w1, v2, v3, w4, twiddle = tables
    results = []
    for c in range(2):
        channel = first_channel + c
        for i in range(2):
            values = x[i, channel].astype(F32)
            for n in range(RB):
                turn[c, i, pl.ds(n, 4, stride=RB), :] = values[:, n * RA : (n + 1) * RA]
        columns = [
            jnp.concatenate(
                [turn[c, i, p * RB : (p + 1) * RB, :] for i in range(2)], axis=0
            ).astype(BF16)
            for p in range(4)
        ]
        current = dot(w1[...], jnp.concatenate(columns, axis=1))
        rows = []
        for p in range(4):
            part = current[:, p * RA : (p + 1) * RA]
            pair = scaled(part[:RB], part[RB:], twiddle[0], -twiddle[1])
            rows.append(jnp.concatenate(pair, axis=1).astype(BF16))
        current = dot(jnp.concatenate(rows, axis=0), v2[...])
        rows = []
        for p in range(4):
            part = current[p * RB : (p + 1) * RB]
            pair = scaled(part[:, :RA], part[:, RA:], spectrum[0], spectrum[1])
            rows.append(jnp.concatenate(pair, axis=1).astype(BF16))
        current = dot(jnp.concatenate(rows, axis=0), v3[...])
        parts = []
        for p in range(4):
            part = current[p * RB : (p + 1) * RB]
            parts.append(scaled(part[:, :RA], part[:, RA:], twiddle[0], twiddle[1]))
        results.append(
            jnp.concatenate([parts[p][i] for i in range(2) for p in range(4)], axis=0).astype(BF16)
        )
    current = dot(w4[...], jnp.concatenate(results, axis=1))
    lane_group = lax.broadcasted_iota(jnp.int32, (N_RG * 8, RA), 1) // OV
    edge = rim[...] if inner else None
    for c in range(2):
        turned = current[:, c * RA : (c + 1) * RA].reshape(N_RG, 2, 8, RA)
        for half in range(2):
            sent[:, unit_of(first_channel + c, half)] = turned[:, half].astype(BF16)
        low = turned[:, 0].reshape(N_RG * 8, RA)
        spot = 2 * inner + c
        if spot:
            edge = jnp.where(lane_group == spot, pltpu.roll(low, OV * spot, 1), edge)
        else:
            edge = low
    if not inner:
        rim[...] = edge
        return
    unit = edge_unit(first_channel // 4)
    kept = edge.astype(BF16).reshape(N_RG, 8, RA)
    sent[0 : N_RG - 1, unit] = kept[1:]
    sent[N_RG - 1, unit] = jnp.zeros((8, RA), BF16)


def sine_cosine(angle):
    turns = angle * (2.0 / math.pi)
    quarter = (turns + 0.5).astype(jnp.int32)
    rest = (turns - quarter.astype(F32)) * (0.5 * math.pi)
    square = rest * rest
    sine = -1.9515295891e-4 * square + 8.3321608736e-3
    sine = sine * square - 1.6666654611e-1
    sine = sine * square * rest + rest
    cosine = 2.443315711809948e-5 * square - 1.388731625493765e-3
    cosine = cosine * square + 4.166664568298827e-2
    cosine = cosine * square * square - 0.5 * square + 1.0
    swap = quarter % 2 == 1
    real = jnp.where(swap, sine, cosine)
    imag = jnp.where(swap, cosine, sine)
    real = jnp.where((quarter + 1) % 4 >= 2, -real, real)
    imag = jnp.where(quarter % 4 >= 2, -imag, imag)
    return real, imag


def build_matrix(bank, spread, matrix):
    same = (
        lax.broadcasted_iota(jnp.int32, (M, M), 0) % GROUP
        == lax.broadcasted_iota(jnp.int32, (M, M), 1) % GROUP
    )
    for n in range(2 * CH):
        wide = lax.dot_general(
            bank[...],
            spread[:, n * M : (n + 1) * M],
            (((0,), (0,)), ((), ())),
            preferred_element_type=F32,
        )
        wide = jnp.where(same, wide, 0.0).astype(BF16)
        matrix[:, n * GROUP : (n + 1) * GROUP, :] = wide.reshape(BLOCKS, GROUP, M)


def build_phases(g, half, rate, width, migration, phase, place):
    cols = slice(half * RA, (half + 1) * RA)
    row = lax.broadcasted_iota(jnp.int32, (GROUP, RA), 0)
    lane = lax.broadcasted_iota(jnp.int32, (GROUP, RA), 1)
    for j in range(CH):
        centered = row + (g * GROUP + (j * M if j < CH // 2 else j * M - CH * M))
        level = (centered * centered) // (CH * M // 2)
        normal = centered.astype(F32) * (1.0 / (CH * M))
        offsets = (migration[:, cols] * level) // (CH * M // 2)
        place[half, g, j] = lane + offsets
        real, imag = sine_cosine(rate[:, cols] * (normal * normal))
        inside = jnp.abs(centered) < width[:, cols]
        phase[half, g, 2 * j] = jnp.where(inside, real, 0.0)
        phase[half, g, 2 * j + 1] = jnp.where(inside, imag, 0.0)


def gathered(held, unit):
    return held[:, unit].astype(F32).reshape(2 * M, RA).astype(BF16)


def forward_pair(channel, half, held, forward, doppler):
    units = [unit_of(channel + n, half) for n in range(2)]
    pulses = jnp.concatenate([gathered(held, unit) for unit in units], axis=1)
    bins = dot(forward[...], pulses).astype(BF16)
    for n in range(2):
        for o in range(2):
            doppler[half, :, 2 * (channel + n) + o] = bins[
                o * M : (o + 1) * M, n * RA : (n + 1) * RA
            ].reshape(BLOCKS, GROUP, RA)


def forward_edges(held, forward, doppler):
    pulses = jnp.concatenate([gathered(held, edge_unit(n)) for n in range(2)], axis=1)
    bins = dot(forward[...], pulses)
    for channel in range(CH):
        group, inner = channel // 4, channel % 4
        part = bins[:, group * RA : (group + 1) * RA]
        if inner:
            part = pltpu.roll(part, RA - OV * inner, 1)
        part = part.astype(BF16)
        for o in range(2):
            doppler[2, :, 2 * channel + o] = part[o * M : (o + 1) * M].reshape(BLOCKS, GROUP, RA)


def correct(g, half, matrix, doppler, bands, phase, place, merge, merged):
    low = doppler[half, g].reshape(M, RA)
    if half:
        both = dot(matrix[g], jnp.concatenate([low, doppler[2, g].reshape(M, RA)], axis=1))
        near, far = both[:, :RA], both[:, RA:]
    else:
        near = dot(matrix[g], low)
    rows = []
    for j in range(CH):
        spot = place[half, g, j]
        here = spot < RA
        spot = spot % RA
        before = place[0, g, j] % RA
        pair = []
        for part in (2 * j, 2 * j + 1):
            at = slice(part * GROUP, (part + 1) * GROUP)
            if half:
                other = jnp.take_along_axis(far[at], spot, axis=1)
                bands[g, at, :] = jnp.take_along_axis(near[at], before, axis=1)
            else:
                other = bands[g, at, :]
            pair.append(jnp.where(here, jnp.take_along_axis(near[at], spot, axis=1), other))
        real, imag = scaled(*pair, phase[half, g, 2 * j], phase[half, g, 2 * j + 1])
        rows += [real.astype(BF16), imag.astype(BF16)]
    mixed = dot(merge[...], jnp.concatenate(rows, axis=0)).astype(BF16)
    merged[:, :, g] = mixed.reshape(CH, 2, GROUP, RA)


def invert(q, inverse, merged, image):
    part = dot(inverse[q], merged[q].reshape(2 * M, RA))
    for o in range(2):
        image[pl.ds(o * CH * RA + q, RA, stride=CH), :] = part[o * RA : (o + 1) * RA]


def focus_kernel(
    x_hbm,
    replica_hbm,
    w1_hbm,
    v2_hbm,
    v3_hbm,
    twiddle_hbm,
    w4_hbm,
    bank_hbm,
    spread_hbm,
    rate_hbm,
    width_hbm,
    migration_hbm,
    forward_hbm,
    merge_hbm,
    inverse_hbm,
    out_hbm,
    x,
    replica,
    w1,
    v2,
    v3,
    twiddle,
    w4,
    bank,
    spread,
    rate,
    width,
    migration,
    forward,
    merge,
    inverse,
    natural,
    spectrum,
    turn,
    rim,
    sent,
    held,
    matrix,
    doppler,
    bands,
    phase,
    place,
    merged,
    image,
    result,
    x_sem,
    table_sem,
    far_send,
    far_recv,
    near_send,
    near_recv,
    own_sem,
    out_sem,
):
    block = lax.axis_index("az")
    me = lax.axis_index("rg")
    px, pz, core = me // 8, (me // 2) % 4, me % 2
    above, below = (block + 1) % N_AZ, (block + N_AZ - 1) % N_AZ

    peers = [
        (px + x) % 4 * 8 + (pz + z) % 4 * 2 + (core + c) % 2
        for x, z in FAR_FIRST
        for c in range(2)
        if (x, z, c) != (0, 0, 0)
    ]

    fetches = [
        pltpu.make_async_copy(x_hbm.at[:, pl.ds(2 * n, 2)], x.at[:, pl.ds(2 * n, 2)], x_sem.at[n])
        for n in range(4)
    ]
    sources = [replica_hbm, w1_hbm, v2_hbm, v3_hbm, twiddle_hbm, w4_hbm, bank_hbm, spread_hbm]
    sources += [rate_hbm, width_hbm, migration_hbm, forward_hbm, merge_hbm, inverse_hbm]
    targets = [replica, w1, v2, v3, twiddle, w4, bank, spread]
    targets += [rate, width, migration, forward, merge, inverse]
    tables = [
        pltpu.make_async_copy(source, target, table_sem.at[n])
        for n, (source, target) in enumerate(zip(sources, targets))
    ]
    for copy in fetches[:1] + tables[:6] + fetches[1:] + tables[6:]:
        copy.start()

    barrier = pltpu.get_barrier_semaphore()

    for target in peers:
        pl.semaphore_signal(barrier, inc=1, device_id=(block, target), device_id_type=MESH)

    for other in (above, below):
        pl.semaphore_signal(barrier, inc=1, device_id=(other, me), device_id_type=MESH)

    own = [
        pltpu.make_async_copy(
            sent.at[me, pl.ds(low, high - low)],
            held.at[16 + me, pl.ds(low, high - low)],
            own_sem.at[n],
        )
        for n, (low, high) in enumerate(CUTS)
    ]

    def send(n):
        low, high = CUTS[n]
        units = pl.ds(low, high - low)

        for target in peers:
            pltpu.make_async_remote_copy(
                src_ref=sent.at[target, units],
                dst_ref=held.at[16 + me, units],
                send_sem=far_send.at[n],
                recv_sem=far_recv.at[n],
                device_id=(block, target),
                device_id_type=MESH,
            ).start()

        own[n].start()

    def onward(n, up):
        low, high = CUTS[n]
        units = pl.ds(low, high - low)
        return pltpu.make_async_remote_copy(
            src_ref=held.at[pl.ds(32 if up else 16, 16), units],
            dst_ref=held.at[pl.ds(0 if up else 48, 16), units],
            send_sem=near_send.at[int(up), n],
            recv_sem=near_recv.at[int(up), n],
            device_id=(above if up else below, me),
            device_id_type=MESH,
        )

    def relay(n):
        low, high = CUTS[n]
        whole = held.at[pl.ds(16, N_RG - 1), pl.ds(low, high - low)]
        pltpu.make_async_copy(whole, whole, far_recv.at[n]).wait()
        own[n].wait()

        @pl.when(block < N_AZ - 1)
        def _():
            onward(n, True).start()

        @pl.when(block > 0)
        def _():
            onward(n, False).start()

    def arrive(n):
        @pl.when(block < N_AZ - 1)
        def _():
            onward(n, False).wait_recv()

        @pl.when(block > 0)
        def _():
            onward(n, True).wait_recv()

    tables[0].wait()
    load_spectrum(replica, natural, spectrum)
    small = (w1, v2, v3, w4, twiddle)
    for n in range(4):
        fetches[n].wait()
        if n == 0:
            for copy in tables[1:6]:
                copy.wait()
        compress_pair(2 * n, n % 2, x, small, spectrum, turn, rim, sent)
        if n == 0:
            pl.semaphore_wait(barrier, N_RG + 1)
        send(n)
    for chunk in range(4, len(CUTS)):
        send(chunk)

    @pl.when(block == 0)
    def _():
        held[0:16] = jnp.zeros((16, UNITS, 8, RA), BF16)

    @pl.when(block == N_AZ - 1)
    def _():
        held[48:64] = jnp.zeros((16, UNITS, 8, RA), BF16)

    def phases(half, low, high):
        @pl.loop(low, high)
        def _(g):
            build_phases(g, half, rate, width, migration, phase, place)

    writes = [
        pltpu.make_async_copy(
            result.at[half], out_hbm.at[:, :, pl.ds(half * RA, RA)], out_sem.at[half]
        )
        for half in range(2)
    ]

    def complete(half):
        for g in range(BLOCKS):
            correct(g, half, matrix, doppler, bands, phase, place, merge, merged)
        for q in range(CH):
            invert(q, inverse, merged, image)

        result[half] = image[...].astype(BF16).reshape(2, CH * RA, RA)
        writes[half].start()

    def forward_chunk(n):
        arrive(n)
        if n == 4:
            forward_edges(held, forward, doppler)
        else:
            forward_pair(2 * (n % 5), int(n < 4), held, forward, doppler)

    relay(0)
    for copy in tables[6:11]:
        copy.wait()
    build_matrix(bank, spread, matrix)
    relay(1)
    phases(1, 0, 8)
    relay(2)
    phases(1, 8, 16)
    relay(3)
    phases(0, 0, 8)
    relay(4)
    phases(0, 8, 16)
    for copy in tables[11:]:
        copy.wait()
    relay(5)
    forward_chunk(0)
    forward_chunk(1)
    relay(6)
    forward_chunk(2)
    forward_chunk(3)
    relay(7)
    forward_chunk(4)
    relay(8)
    complete(1)
    for n in range(5, len(CUTS)):
        forward_chunk(n)
    complete(0)

    for n, (low, high) in enumerate(CUTS):
        whole = held.at[pl.ds(16, N_RG - 1), pl.ds(low, high - low)]
        pltpu.make_async_copy(whole, whole, far_send.at[n]).wait()

        @pl.when(block < N_AZ - 1)
        def _():
            onward(n, True).wait_send()

        @pl.when(block > 0)
        def _():
            onward(n, False).wait_send()

    for copy in writes:
        copy.wait()


def shards(echoes, replica, filter_bank, doppler_rate, doppler_width, migration):
    w1, v2, v3, w4, twiddle = range_tables()
    forward, inverse, merge, spread = azimuth_tables()
    operands = [echoes, replica]
    operands += [jnp.asarray(t) for t in (w1, v2, v3, twiddle, w4)]
    operands += [filter_bank.reshape(2 * CH * CH, M), jnp.asarray(spread)]
    operands += [a.reshape(1, 2 * RA) for a in (doppler_rate, doppler_width, migration)]
    operands += [jnp.asarray(t) for t in (forward, merge, inverse)]
    hbm = pl.BlockSpec(memory_space=pl.ANY)
    count = len(CUTS)
    return pl.pallas_call(
        focus_kernel,
        out_shape=jax.ShapeDtypeStruct((2, CH * RA, 2 * RA), BF16),
        in_specs=[hbm] * 15,
        out_specs=hbm,
        scratch_shapes=[
            pltpu.VMEM((2, CH, 4, R), BF16),
            *[pltpu.VMEM(o.shape, o.dtype) for o in operands[1:]],
            pltpu.VMEM((2 * RB, RA), F32),
            pltpu.VMEM((2, RB, RA), F32),
            pltpu.VMEM((2, 2, 4 * RB, RA), F32),
            pltpu.VMEM((N_RG * 8, RA), F32),
            pltpu.VMEM((N_RG, UNITS, 8, RA), BF16),
            pltpu.VMEM((2 * N_RG, UNITS, 8, RA), BF16),
            pltpu.VMEM((BLOCKS, M, M), BF16),
            pltpu.VMEM((3, BLOCKS, 2 * CH, GROUP, RA), BF16),
            pltpu.VMEM((BLOCKS, M, RA), F32),
            pltpu.VMEM((2, BLOCKS, 2 * CH, GROUP, RA), F32),
            pltpu.VMEM((2, BLOCKS, CH, GROUP, RA), jnp.int32),
            pltpu.VMEM((CH, 2, BLOCKS, GROUP, RA), BF16),
            pltpu.VMEM((2 * CH * RA, RA), F32),
            pltpu.VMEM((2, 2, CH * RA, RA), BF16),
            pltpu.SemaphoreType.DMA((4,)),
            pltpu.SemaphoreType.DMA((14,)),
            pltpu.SemaphoreType.DMA((count,)),
            pltpu.SemaphoreType.DMA((count,)),
            pltpu.SemaphoreType.DMA((2, count)),
            pltpu.SemaphoreType.DMA((2, count)),
            pltpu.SemaphoreType.DMA((count,)),
            pltpu.SemaphoreType.DMA((2,)),
        ],
        compiler_params=pltpu.CompilerParams(
            collective_id=0, has_side_effects=True, vmem_limit_bytes=60 * 2**20
        ),
        cost_estimate=pl.CostEstimate(
            flops=2 * 2_000_000_000, bytes_accessed=2**23, transcendentals=0
        ),
        name="focus",
    )(*operands)


def solution(mesh):
    placed = (P(None, None, ("az", "rg"), None), P(), P(), P("rg"), P("rg"), P("rg"))
    return jax.shard_map(
        shards, mesh=mesh, in_specs=placed, out_specs=P(None, "az", "rg"), check_vma=False
    )
```

```python
import functools
import math

import jax
import jax.numpy as jnp
import ml_dtypes
import numpy as np
from jax import lax
from jax.experimental import pallas as pl
from jax.experimental.pallas import tpu as pltpu
from jax.sharding import PartitionSpec as P

CH = 8
RA = 128
RB = 64
R = RA * RB
M = 256
E = 64
OV = 32
N_AZ = 4
N_RG = 32
GROUP = 16
BLOCKS = M // GROUP
UNITS = 18
CUTS = tuple((n, n + 2) for n in range(0, UNITS, 2))
FAR_FIRST = ((2, 2), (1, 2), (2, 1), (3, 2), (2, 3), (1, 1), (3, 3), (1, 3), (3, 1))
FAR_FIRST += ((2, 0), (0, 2), (1, 0), (0, 1), (3, 0), (0, 3), (0, 0))
MESH = pl.DeviceIdType.MESH
F32 = jnp.float32
BF16 = jnp.bfloat16


def stored(table):
    return np.asarray(table, np.float32).astype(ml_dtypes.bfloat16)


def angle_pair(product, length):
    angles = 2.0 * math.pi / length * (np.asarray(product) % length)
    return np.cos(angles), np.sin(angles)


def real_rows(cosine, sine):
    return np.stack(
        [np.stack([cosine, -sine], axis=1), np.stack([sine, cosine], axis=1)]
    )


def unit_of(channel, half):
    return channel if half else 10 + channel


def edge_unit(group):
    return CH + group


def range_tables():
    ids = np.arange(RB)
    cosine, sine = angle_pair(ids[:, None] * ids[None, :], RB)
    w1 = real_rows(cosine, -sine).reshape(2 * RB, 2 * RB)
    w4 = real_rows(cosine, sine) / R
    w4 = np.einsum("obik,pn->bopink", w4, np.eye(4)).reshape(8 * RB, 8 * RB)
    ids = np.arange(RA)
    order = 2 * (ids % RB) + ids // RB
    cosine, sine = angle_pair(ids[:, None] * ids[None, :], RA)
    v2 = real_rows(cosine, -sine)[:, order].reshape(2 * RA, 2 * RA).T
    v3 = real_rows(cosine, sine)[..., order].reshape(2 * RA, 2 * RA).T
    cosine, sine = angle_pair(np.arange(RB)[:, None] * np.arange(RA)[None, :], R)
    twiddle = np.stack([cosine, sine]).astype(np.float32)
    return stored(w1), stored(v2), stored(v3), stored(w4), twiddle


def azimuth_tables():
    freqs = np.arange(M)
    cosine, sine = angle_pair(freqs[:, None] * np.arange(M)[None, :], M)
    forward = real_rows(cosine, -sine)
    forward = forward.reshape(2, M, 2, M // 4, 4).transpose(0, 1, 3, 2, 4).reshape(2 * M, 2 * M)
    slots = np.arange(E, M - E)
    inverse = []
    for q in range(CH):
        cosine, sine = angle_pair((CH * slots[:, None] + q) * freqs[None, :], CH * M)
        inverse.append(real_rows(cosine, sine).reshape(M, 2 * M) / (CH * M))
    ids = np.arange(CH)
    cosine, sine = angle_pair(ids[:, None] * ids[None, :], CH)
    merge = real_rows(cosine, sine).transpose(1, 0, 2, 3)
    merge = merge.transpose(0, 1, 3, 2).reshape(2 * CH, 2 * CH)
    merge = np.kron(merge, np.eye(GROUP))
    spread = np.zeros((2, CH, CH, CH, 2, CH, 2, GROUP))
    for j in range(CH):
        for c in range(CH):
            spread[0, j, c, j, 0, c, 0] = 1.0
            spread[1, j, c, j, 0, c, 1] = -1.0
            spread[1, j, c, j, 1, c, 0] = 1.0
            spread[0, j, c, j, 1, c, 1] = 1.0
    spread = spread.reshape(2 * CH * CH, 2 * CH * 2 * CH * GROUP)
    return stored(forward), stored(np.stack(inverse)), stored(merge), stored(spread)


def dot(a, b):
    return jnp.dot(a, b, preferred_element_type=F32)


def scaled(real, imag, table_real, table_imag):
    return (
        real * table_real - imag * table_imag,
        real * table_imag + imag * table_real,
    )


def load_spectrum(replica, natural, spectrum):
    values = replica[...]
    for n in range(RB):
        natural[pl.ds(n, 2, stride=RB), :] = values[:, n * RA : (n + 1) * RA]
    turned = natural[...].T
    for i in range(2):
        part = turned[:, i * RB : (i + 1) * RB]
        spectrum[i] = jnp.concatenate([part[:RB], part[RB:]], axis=1)


def compress_pair(first_channel, inner, x, tables, spectrum, turn, rim, sent):
    w1, v2, v3, w4, twiddle = tables
    results = []
    for c in range(2):
        channel = first_channel + c
        for i in range(2):
            values = x[i, channel].astype(F32)
            for n in range(RB):
                turn[c, i, pl.ds(n, 4, stride=RB), :] = values[:, n * RA : (n + 1) * RA]
        columns = [
            jnp.concatenate(
                [turn[c, i, p * RB : (p + 1) * RB, :] for i in range(2)], axis=0
            ).astype(BF16)
            for p in range(4)
        ]
        current = dot(w1[...], jnp.concatenate(columns, axis=1))
        rows = []
        for p in range(4):
            part = current[:, p * RA : (p + 1) * RA]
            pair = scaled(part[:RB], part[RB:], twiddle[0], -twiddle[1])
            rows.append(jnp.concatenate(pair, axis=1).astype(BF16))
        current = dot(jnp.concatenate(rows, axis=0), v2[...])
        rows = []
        for p in range(4):
            part = current[p * RB : (p + 1) * RB]
            pair = scaled(part[:, :RA], part[:, RA:], spectrum[0], spectrum[1])
            rows.append(jnp.concatenate(pair, axis=1).astype(BF16))
        current = dot(jnp.concatenate(rows, axis=0), v3[...])
        parts = []
        for p in range(4):
            part = current[p * RB : (p + 1) * RB]
            parts.append(scaled(part[:, :RA], part[:, RA:], twiddle[0], twiddle[1]))
        results.append(
            jnp.concatenate([parts[p][i] for i in range(2) for p in range(4)], axis=0).astype(BF16)
        )
    current = dot(w4[...], jnp.concatenate(results, axis=1))
    lane_group = lax.broadcasted_iota(jnp.int32, (N_RG * 8, RA), 1) // OV
    edge = rim[...] if inner else None
    for c in range(2):
        turned = current[:, c * RA : (c + 1) * RA].reshape(N_RG, 2, 8, RA)
        for half in range(2):
            sent[:, unit_of(first_channel + c, half)] = turned[:, half].astype(BF16)
        low = turned[:, 0].reshape(N_RG * 8, RA)
        spot = 2 * inner + c
        if spot:
            edge = jnp.where(lane_group == spot, pltpu.roll(low, OV * spot, 1), edge)
        else:
            edge = low
    if not inner:
        rim[...] = edge
        return
    unit = edge_unit(first_channel // 4)
    kept = edge.astype(BF16).reshape(N_RG, 8, RA)
    sent[0 : N_RG - 1, unit] = kept[1:]
    sent[N_RG - 1, unit] = jnp.zeros((8, RA), BF16)


def sine_cosine(angle):
    turns = angle * (2.0 / math.pi)
    quarter = (turns + 0.5).astype(jnp.int32)
    rest = (turns - quarter.astype(F32)) * (0.5 * math.pi)
    square = rest * rest
    sine = -1.9515295891e-4 * square + 8.3321608736e-3
    sine = sine * square - 1.6666654611e-1
    sine = sine * square * rest + rest
    cosine = 2.443315711809948e-5 * square - 1.388731625493765e-3
    cosine = cosine * square + 4.166664568298827e-2
    cosine = cosine * square * square - 0.5 * square + 1.0
    swap = (quarter & 1) == 1
    real = jnp.where(swap, sine, cosine)
    imag = jnp.where(swap, cosine, sine)
    real = jnp.where(((quarter + 1) & 2) == 2, -real, real)
    imag = jnp.where((quarter & 2) == 2, -imag, imag)
    return real, imag


def build_matrix(bank, spread, matrix):
    same = (
        lax.broadcasted_iota(jnp.int32, (M, M), 0) % GROUP
        == lax.broadcasted_iota(jnp.int32, (M, M), 1) % GROUP
    )
    for n in range(2 * CH):
        wide = lax.dot_general(
            bank[...],
            spread[:, n * M : (n + 1) * M],
            (((0,), (0,)), ((), ())),
            preferred_element_type=F32,
        )
        wide = jnp.where(same, wide, 0.0).astype(BF16)
        matrix[:, n * GROUP : (n + 1) * GROUP, :] = wide.reshape(BLOCKS, GROUP, M)


def build_phases(g, half, rate, width, migration, phase, place):
    cols = slice(half * RA, (half + 1) * RA)
    row = lax.broadcasted_iota(jnp.int32, (GROUP, RA), 0)
    lane = lax.broadcasted_iota(jnp.int32, (GROUP, RA), 1)
    row = (row + g * GROUP).astype(F32)
    scale = 2.0 / (CH * M)
    per_level = jnp.broadcast_to(migration[:, cols].astype(F32) * scale, (GROUP, RA))
    rates = jnp.broadcast_to(rate[:, cols], (GROUP, RA))
    widths = jnp.broadcast_to(width[:, cols].astype(F32), (GROUP, RA))
    for j in range(CH):
        centered = row + float(j * M if j < CH // 2 else j * M - CH * M)
        square = centered * centered
        offsets = (per_level * jnp.floor(square * scale)).astype(jnp.int32)
        place[half, g, j] = lane + offsets
        real, imag = sine_cosine(rates * (square * (1.0 / (CH * M) ** 2)))
        inside = jnp.abs(centered) < widths
        phase[half, g, 2 * j] = jnp.where(inside, real, 0.0)
        phase[half, g, 2 * j + 1] = jnp.where(inside, imag, 0.0)


def gathered(held, unit):
    return held[:, unit].astype(F32).reshape(2 * M, RA).astype(BF16)


def forward_pair(channel, half, held, forward, doppler):
    units = [unit_of(channel + n, half) for n in range(2)]
    pulses = jnp.concatenate([gathered(held, unit) for unit in units], axis=1)
    bins = dot(forward[...], pulses).astype(BF16)
    for n in range(2):
        for o in range(2):
            doppler[half, :, 2 * (channel + n) + o] = bins[
                o * M : (o + 1) * M, n * RA : (n + 1) * RA
            ].reshape(BLOCKS, GROUP, RA)


def forward_edges(held, forward, doppler):
    pulses = jnp.concatenate([gathered(held, edge_unit(n)) for n in range(2)], axis=1)
    bins = dot(forward[...], pulses)
    for channel in range(CH):
        group, inner = channel // 4, channel % 4
        part = bins[:, group * RA : (group + 1) * RA]
        if inner:
            part = pltpu.roll(part, RA - OV * inner, 1)
        part = part.astype(BF16)
        for o in range(2):
            doppler[2, :, 2 * channel + o] = part[o * M : (o + 1) * M].reshape(BLOCKS, GROUP, RA)


def correct(g, half, matrix, doppler, bands, phase, place, merge, merged):
    low = doppler[half, g].reshape(M, RA)
    if half:
        both = dot(matrix[g], jnp.concatenate([low, doppler[2, g].reshape(M, RA)], axis=1))
        near, far = both[:, :RA], both[:, RA:]
    else:
        near = dot(matrix[g], low)
    rows = []
    for j in range(CH):
        spot = place[half, g, j]
        here = spot < RA
        spot = spot & (RA - 1)
        before = place[0, g, j] & (RA - 1)
        pair = []
        for part in (2 * j, 2 * j + 1):
            at = slice(part * GROUP, (part + 1) * GROUP)
            if half:
                other = jnp.take_along_axis(far[at], spot, axis=1)
                bands[g, at, :] = jnp.take_along_axis(near[at], before, axis=1)
            else:
                other = bands[g, at, :]
            pair.append(jnp.where(here, jnp.take_along_axis(near[at], spot, axis=1), other))
        real, imag = scaled(*pair, phase[half, g, 2 * j], phase[half, g, 2 * j + 1])
        rows += [real.astype(BF16), imag.astype(BF16)]
    mixed = dot(merge[...], jnp.concatenate(rows, axis=0)).astype(BF16)
    merged[:, :, g] = mixed.reshape(CH, 2, GROUP, RA)


def invert(q, inverse, merged, image):
    part = dot(inverse[q], merged[q].reshape(2 * M, RA))
    for o in range(2):
        image[pl.ds(o * CH * RA + q, RA, stride=CH), :] = part[o * RA : (o + 1) * RA]


def focus_kernel(
    x_hbm,
    replica_hbm,
    w1_hbm,
    v2_hbm,
    v3_hbm,
    twiddle_hbm,
    w4_hbm,
    bank_hbm,
    spread_hbm,
    rate_hbm,
    width_hbm,
    migration_hbm,
    forward_hbm,
    merge_hbm,
    inverse_hbm,
    out_hbm,
    x,
    replica,
    w1,
    v2,
    v3,
    twiddle,
    w4,
    bank,
    spread,
    rate,
    width,
    migration,
    forward,
    merge,
    inverse,
    natural,
    spectrum,
    turn,
    rim,
    sent,
    held,
    matrix,
    doppler,
    bands,
    phase,
    place,
    merged,
    image,
    result,
    x_sem,
    table_sem,
    far_send,
    far_recv,
    near_send,
    near_recv,
    own_sem,
    out_sem,
):
    block = lax.axis_index("az")
    me = lax.axis_index("rg")
    px, pz, core = me // 8, (me // 2) % 4, me % 2
    above, below = (block + 1) % N_AZ, (block + N_AZ - 1) % N_AZ

    peers = [
        (px + x) % 4 * 8 + (pz + z) % 4 * 2 + (core + c) % 2
        for x, z in FAR_FIRST
        for c in range(2)
        if (x, z, c) != (0, 0, 0)
    ]

    fetches = [
        pltpu.make_async_copy(x_hbm.at[:, pl.ds(2 * n, 2)], x.at[:, pl.ds(2 * n, 2)], x_sem.at[n])
        for n in range(4)
    ]
    sources = [replica_hbm, w1_hbm, v2_hbm, v3_hbm, twiddle_hbm, w4_hbm, bank_hbm, spread_hbm]
    sources += [rate_hbm, width_hbm, migration_hbm, forward_hbm, merge_hbm, inverse_hbm]
    targets = [replica, w1, v2, v3, twiddle, w4, bank, spread]
    targets += [rate, width, migration, forward, merge, inverse]
    tables = [
        pltpu.make_async_copy(source, target, table_sem.at[n])
        for n, (source, target) in enumerate(zip(sources, targets))
    ]
    for copy in fetches[:1] + tables[:6] + fetches[1:] + tables[6:]:
        copy.start()

    barrier = pltpu.get_barrier_semaphore()

    for target in peers:
        pl.semaphore_signal(barrier, inc=1, device_id=(block, target), device_id_type=MESH)

    for other in (above, below):
        pl.semaphore_signal(barrier, inc=1, device_id=(other, me), device_id_type=MESH)

    own = [
        pltpu.make_async_copy(
            sent.at[me, pl.ds(low, high - low)],
            held.at[16 + me, pl.ds(low, high - low)],
            own_sem.at[n],
        )
        for n, (low, high) in enumerate(CUTS)
    ]

    def send(n):
        low, high = CUTS[n]
        units = pl.ds(low, high - low)

        for target in peers:
            pltpu.make_async_remote_copy(
                src_ref=sent.at[target, units],
                dst_ref=held.at[16 + me, units],
                send_sem=far_send.at[n],
                recv_sem=far_recv.at[n],
                device_id=(block, target),
                device_id_type=MESH,
            ).start()

        own[n].start()

    def onward(n, up):
        low, high = CUTS[n]
        units = pl.ds(low, high - low)
        return pltpu.make_async_remote_copy(
            src_ref=held.at[pl.ds(32 if up else 16, 16), units],
            dst_ref=held.at[pl.ds(0 if up else 48, 16), units],
            send_sem=near_send.at[int(up), n],
            recv_sem=near_recv.at[int(up), n],
            device_id=(above if up else below, me),
            device_id_type=MESH,
        )

    def relay(n):
        low, high = CUTS[n]
        whole = held.at[pl.ds(16, N_RG - 1), pl.ds(low, high - low)]
        pltpu.make_async_copy(whole, whole, far_recv.at[n]).wait()
        own[n].wait()

        @pl.when(block < N_AZ - 1)
        def _():
            onward(n, True).start()

        @pl.when(block > 0)
        def _():
            onward(n, False).start()

    def arrive(n):
        @pl.when(block < N_AZ - 1)
        def _():
            onward(n, False).wait_recv()

        @pl.when(block > 0)
        def _():
            onward(n, True).wait_recv()

    tables[0].wait()
    load_spectrum(replica, natural, spectrum)
    small = (w1, v2, v3, w4, twiddle)
    for n in range(4):
        fetches[n].wait()
        if n == 0:
            for copy in tables[1:6]:
                copy.wait()
        compress_pair(2 * n, n % 2, x, small, spectrum, turn, rim, sent)
        if n == 0:
            pl.semaphore_wait(barrier, N_RG + 1)
        send(n)
    for chunk in range(4, len(CUTS)):
        send(chunk)

    @pl.when(block == 0)
    def _():
        held[0:16] = jnp.zeros((16, UNITS, 8, RA), BF16)

    @pl.when(block == N_AZ - 1)
    def _():
        held[48:64] = jnp.zeros((16, UNITS, 8, RA), BF16)

    def phases(half, low, high):
        @pl.loop(low, high)
        def _(g):
            build_phases(g, half, rate, width, migration, phase, place)

    writes = [
        pltpu.make_async_copy(
            result.at[half], out_hbm.at[:, :, pl.ds(half * RA, RA)], out_sem.at[half]
        )
        for half in range(2)
    ]

    def complete(half):
        for g in range(BLOCKS):
            correct(g, half, matrix, doppler, bands, phase, place, merge, merged)
        for q in range(CH):
            invert(q, inverse, merged, image)

        result[half] = image[...].astype(BF16).reshape(2, CH * RA, RA)
        writes[half].start()

    def forward_chunk(n):
        arrive(n)
        if n == 4:
            forward_edges(held, forward, doppler)
        else:
            forward_pair(2 * (n % 5), int(n < 4), held, forward, doppler)

    relay(0)
    for copy in tables[6:11]:
        copy.wait()
    build_matrix(bank, spread, matrix)
    relay(1)
    phases(1, 0, 8)
    relay(2)
    phases(1, 8, 16)
    relay(3)
    phases(0, 0, 8)
    relay(4)
    phases(0, 8, 16)
    for copy in tables[11:]:
        copy.wait()
    relay(5)
    forward_chunk(0)
    forward_chunk(1)
    relay(6)
    forward_chunk(2)
    forward_chunk(3)
    relay(7)
    forward_chunk(4)
    relay(8)
    complete(1)
    for n in range(5, len(CUTS)):
        forward_chunk(n)
    complete(0)

    for n, (low, high) in enumerate(CUTS):
        whole = held.at[pl.ds(16, N_RG - 1), pl.ds(low, high - low)]
        pltpu.make_async_copy(whole, whole, far_send.at[n]).wait()

        @pl.when(block < N_AZ - 1)
        def _():
            onward(n, True).wait_send()

        @pl.when(block > 0)
        def _():
            onward(n, False).wait_send()

    for copy in writes:
        copy.wait()


def shards(echoes, replica, filter_bank, doppler_rate, doppler_width, migration):
    w1, v2, v3, w4, twiddle = range_tables()
    forward, inverse, merge, spread = azimuth_tables()
    operands = [echoes, replica]
    operands += [jnp.asarray(t) for t in (w1, v2, v3, twiddle, w4)]
    operands += [filter_bank.reshape(2 * CH * CH, M), jnp.asarray(spread)]
    operands += [a.reshape(1, 2 * RA) for a in (doppler_rate, doppler_width, migration)]
    operands += [jnp.asarray(t) for t in (forward, merge, inverse)]
    hbm = pl.BlockSpec(memory_space=pl.ANY)
    count = len(CUTS)
    return pl.pallas_call(
        focus_kernel,
        out_shape=jax.ShapeDtypeStruct((2, CH * RA, 2 * RA), BF16),
        in_specs=[hbm] * 15,
        out_specs=hbm,
        scratch_shapes=[
            pltpu.VMEM((2, CH, 4, R), BF16),
            *[pltpu.VMEM(o.shape, o.dtype) for o in operands[1:]],
            pltpu.VMEM((2 * RB, RA), F32),
            pltpu.VMEM((2, RB, RA), F32),
            pltpu.VMEM((2, 2, 4 * RB, RA), F32),
            pltpu.VMEM((N_RG * 8, RA), F32),
            pltpu.VMEM((N_RG, UNITS, 8, RA), BF16),
            pltpu.VMEM((2 * N_RG, UNITS, 8, RA), BF16),
            pltpu.VMEM((BLOCKS, M, M), BF16),
            pltpu.VMEM((3, BLOCKS, 2 * CH, GROUP, RA), BF16),
            pltpu.VMEM((BLOCKS, M, RA), F32),
            pltpu.VMEM((2, BLOCKS, 2 * CH, GROUP, RA), F32),
            pltpu.VMEM((2, BLOCKS, CH, GROUP, RA), jnp.int32),
            pltpu.VMEM((CH, 2, BLOCKS, GROUP, RA), BF16),
            pltpu.VMEM((2 * CH * RA, RA), F32),
            pltpu.VMEM((2, 2, CH * RA, RA), BF16),
            pltpu.SemaphoreType.DMA((4,)),
            pltpu.SemaphoreType.DMA((14,)),
            pltpu.SemaphoreType.DMA((count,)),
            pltpu.SemaphoreType.DMA((count,)),
            pltpu.SemaphoreType.DMA((2, count)),
            pltpu.SemaphoreType.DMA((2, count)),
            pltpu.SemaphoreType.DMA((count,)),
            pltpu.SemaphoreType.DMA((2,)),
        ],
        compiler_params=pltpu.CompilerParams(
            collective_id=0, has_side_effects=True, vmem_limit_bytes=60 * 2**20
        ),
        cost_estimate=pl.CostEstimate(
            flops=2 * 2_000_000_000, bytes_accessed=2**23, transcendentals=0
        ),
        name="focus",
    )(*operands)


def solution(mesh):
    placed = (P(None, None, ("az", "rg"), None), P(), P(), P("rg"), P("rg"), P("rg"))
    return jax.shard_map(
        shards, mesh=mesh, in_specs=placed, out_specs=P(None, "az", "rg"), check_vma=False
    )
```

```python
import functools
import math

import jax
import jax.numpy as jnp
import ml_dtypes
import numpy as np
from jax import lax
from jax.experimental import pallas as pl
from jax.experimental.pallas import tpu as pltpu
from jax.sharding import PartitionSpec as P

CH = 8
RA = 128
RB = 64
R = RA * RB
M = 256
E = 64
OV = 32
N_AZ = 4
N_RG = 32
GROUP = 16
BLOCKS = M // GROUP
UNITS = 18
CUTS = tuple((n, n + 2) for n in range(0, UNITS, 2))
FAR_FIRST = ((2, 2), (1, 2), (2, 1), (3, 2), (2, 3), (1, 1), (3, 3), (1, 3), (3, 1))
FAR_FIRST += ((2, 0), (0, 2), (1, 0), (0, 1), (3, 0), (0, 3), (0, 0))
MESH = pl.DeviceIdType.MESH
F32 = jnp.float32
BF16 = jnp.bfloat16


def stored(table):
    return np.asarray(table, np.float32).astype(ml_dtypes.bfloat16)


def angle_pair(product, length):
    angles = 2.0 * math.pi / length * (np.asarray(product) % length)
    return np.cos(angles), np.sin(angles)


def real_rows(cosine, sine):
    return np.stack(
        [np.stack([cosine, -sine], axis=1), np.stack([sine, cosine], axis=1)]
    )


def unit_of(channel, half):
    return channel if half else 10 + channel


def edge_unit(group):
    return CH + group


def range_tables():
    ids = np.arange(RB)
    cosine, sine = angle_pair(ids[:, None] * ids[None, :], RB)
    w1 = real_rows(cosine, -sine).reshape(2 * RB, 2 * RB)
    w4 = real_rows(cosine, sine) / R
    w4 = np.einsum("obik,pn->bopink", w4, np.eye(4)).reshape(8 * RB, 8 * RB)
    ids = np.arange(RA)
    order = 2 * (ids % RB) + ids // RB
    cosine, sine = angle_pair(ids[:, None] * ids[None, :], RA)
    v2 = real_rows(cosine, -sine)[:, order].reshape(2 * RA, 2 * RA).T
    v3 = real_rows(cosine, sine)[..., order].reshape(2 * RA, 2 * RA).T
    cosine, sine = angle_pair(np.arange(RB)[:, None] * np.arange(RA)[None, :], R)
    twiddle = np.stack([cosine, sine]).astype(np.float32)
    return stored(w1), stored(v2), stored(v3), stored(w4), twiddle


def azimuth_tables():
    freqs = np.arange(M)
    cosine, sine = angle_pair(freqs[:, None] * np.arange(M)[None, :], M)
    forward = real_rows(cosine, -sine)
    forward = forward.reshape(2, M, 2, M // 4, 4).transpose(0, 1, 3, 2, 4).reshape(2 * M, 2 * M)
    slots = np.arange(E, M - E)
    inverse = []
    for q in range(CH):
        cosine, sine = angle_pair((CH * slots[:, None] + q) * freqs[None, :], CH * M)
        inverse.append(real_rows(cosine, sine).reshape(M, 2 * M) / (CH * M))
    ids = np.arange(CH)
    cosine, sine = angle_pair(ids[:, None] * ids[None, :], CH)
    merge = real_rows(cosine, sine).transpose(1, 0, 2, 3)
    merge = merge.transpose(0, 1, 3, 2).reshape(2 * CH, 2 * CH)
    merge = np.kron(merge, np.eye(GROUP))
    spread = np.zeros((2, CH, CH, CH, 2, CH, 2, GROUP))
    for j in range(CH):
        for c in range(CH):
            spread[0, j, c, j, 0, c, 0] = 1.0
            spread[1, j, c, j, 0, c, 1] = -1.0
            spread[1, j, c, j, 1, c, 0] = 1.0
            spread[0, j, c, j, 1, c, 1] = 1.0
    spread = spread.reshape(2 * CH * CH, 2 * CH * 2 * CH * GROUP)
    return stored(forward), stored(np.stack(inverse)), stored(merge), stored(spread)


def dot(a, b):
    return jnp.dot(a, b, preferred_element_type=F32)


def scaled(real, imag, table_real, table_imag):
    return (
        real * table_real - imag * table_imag,
        real * table_imag + imag * table_real,
    )


def load_spectrum(replica, natural, spectrum):
    values = replica[...]
    for n in range(RB):
        natural[pl.ds(n, 2, stride=RB), :] = values[:, n * RA : (n + 1) * RA]
    turned = natural[...].T
    for i in range(2):
        part = turned[:, i * RB : (i + 1) * RB]
        spectrum[i] = jnp.concatenate([part[:RB], part[RB:]], axis=1)


def compress_pair(first_channel, inner, x, tables, spectrum, turn, rim, sent):
    w1, v2, v3, w4, twiddle = tables
    results = []
    for c in range(2):
        channel = first_channel + c
        for i in range(2):
            values = x[i, channel].astype(F32)
            for n in range(RB):
                turn[c, i, pl.ds(n, 4, stride=RB), :] = values[:, n * RA : (n + 1) * RA]
        columns = [
            jnp.concatenate(
                [turn[c, i, p * RB : (p + 1) * RB, :] for i in range(2)], axis=0
            ).astype(BF16)
            for p in range(4)
        ]
        current = dot(w1[...], jnp.concatenate(columns, axis=1))
        rows = []
        for p in range(4):
            part = current[:, p * RA : (p + 1) * RA]
            pair = scaled(part[:RB], part[RB:], twiddle[0], -twiddle[1])
            rows.append(jnp.concatenate(pair, axis=1).astype(BF16))
        current = dot(jnp.concatenate(rows, axis=0), v2[...])
        rows = []
        for p in range(4):
            part = current[p * RB : (p + 1) * RB]
            pair = scaled(part[:, :RA], part[:, RA:], spectrum[0], spectrum[1])
            rows.append(jnp.concatenate(pair, axis=1).astype(BF16))
        current = dot(jnp.concatenate(rows, axis=0), v3[...])
        parts = []
        for p in range(4):
            part = current[p * RB : (p + 1) * RB]
            parts.append(scaled(part[:, :RA], part[:, RA:], twiddle[0], twiddle[1]))
        results.append(
            jnp.concatenate([parts[p][i] for i in range(2) for p in range(4)], axis=0).astype(BF16)
        )
    current = dot(w4[...], jnp.concatenate(results, axis=1))
    lane_group = lax.broadcasted_iota(jnp.int32, (N_RG * 8, RA), 1) // OV
    edge = rim[...] if inner else None
    for c in range(2):
        turned = current[:, c * RA : (c + 1) * RA].reshape(N_RG, 2, 8, RA)
        for half in range(2):
            sent[:, unit_of(first_channel + c, half)] = turned[:, half].astype(BF16)
        low = turned[:, 0].reshape(N_RG * 8, RA)
        spot = 2 * inner + c
        if spot:
            edge = jnp.where(lane_group == spot, pltpu.roll(low, OV * spot, 1), edge)
        else:
            edge = low
    if not inner:
        rim[...] = edge
        return
    unit = edge_unit(first_channel // 4)
    kept = edge.astype(BF16).reshape(N_RG, 8, RA)
    sent[0 : N_RG - 1, unit] = kept[1:]
    sent[N_RG - 1, unit] = jnp.zeros((8, RA), BF16)


def sine_cosine(angle):
    turns = angle * (2.0 / math.pi)
    quarter = (turns + 0.5).astype(jnp.int32)
    rest = (turns - quarter.astype(F32)) * (0.5 * math.pi)
    square = rest * rest
    sine = -1.9515295891e-4 * square + 8.3321608736e-3
    sine = sine * square - 1.6666654611e-1
    sine = sine * square * rest + rest
    cosine = 2.443315711809948e-5 * square - 1.388731625493765e-3
    cosine = cosine * square + 4.166664568298827e-2
    cosine = cosine * square * square - 0.5 * square + 1.0
    swap = (quarter & 1) == 1
    real = jnp.where(swap, sine, cosine)
    imag = jnp.where(swap, cosine, sine)
    real = jnp.where(((quarter + 1) & 2) == 2, -real, real)
    imag = jnp.where((quarter & 2) == 2, -imag, imag)
    return real, imag


def build_matrix(bank, spread, matrix):
    same = (
        lax.broadcasted_iota(jnp.int32, (M, M), 0) % GROUP
        == lax.broadcasted_iota(jnp.int32, (M, M), 1) % GROUP
    )
    for n in range(2 * CH):
        wide = lax.dot_general(
            bank[...],
            spread[:, n * M : (n + 1) * M],
            (((0,), (0,)), ((), ())),
            preferred_element_type=F32,
        )
        wide = jnp.where(same, wide, 0.0).astype(BF16)
        matrix[:, n * GROUP : (n + 1) * GROUP, :] = wide.reshape(BLOCKS, GROUP, M)


def build_phases(g, half, rate, width, migration, phase, place):
    cols = slice(half * RA, (half + 1) * RA)
    row = lax.broadcasted_iota(jnp.int32, (GROUP, RA), 0)
    lane = lax.broadcasted_iota(jnp.int32, (GROUP, RA), 1)
    row = (row + g * GROUP).astype(F32)
    scale = 2.0 / (CH * M)
    per_level = jnp.broadcast_to(migration[:, cols].astype(F32) * scale, (GROUP, RA))
    rates = jnp.broadcast_to(rate[:, cols], (GROUP, RA))
    widths = jnp.broadcast_to(width[:, cols].astype(F32), (GROUP, RA))
    for j in range(CH):
        centered = row + float(j * M if j < CH // 2 else j * M - CH * M)
        square = centered * centered
        offsets = (per_level * jnp.floor(square * scale)).astype(jnp.int32)
        place[half, g, j] = lane + offsets
        real, imag = sine_cosine(rates * (square * (1.0 / (CH * M) ** 2)))
        inside = jnp.abs(centered) < widths
        phase[half, g, 2 * j] = jnp.where(inside, real, 0.0)
        phase[half, g, 2 * j + 1] = jnp.where(inside, imag, 0.0)


def gathered(held, unit):
    return held[:, unit].astype(F32).reshape(2 * M, RA).astype(BF16)


def forward_pair(channel, half, held, forward, doppler):
    units = [unit_of(channel + n, half) for n in range(2)]
    pulses = jnp.concatenate([gathered(held, unit) for unit in units], axis=1)
    bins = dot(forward[...], pulses).astype(BF16)
    for n in range(2):
        for o in range(2):
            doppler[half, :, 2 * (channel + n) + o] = bins[
                o * M : (o + 1) * M, n * RA : (n + 1) * RA
            ].reshape(BLOCKS, GROUP, RA)


def forward_edges(held, forward, doppler):
    pulses = jnp.concatenate([gathered(held, edge_unit(n)) for n in range(2)], axis=1)
    bins = dot(forward[...], pulses)
    for channel in range(CH):
        group, inner = channel // 4, channel % 4
        part = bins[:, group * RA : (group + 1) * RA]
        if inner:
            part = pltpu.roll(part, RA - OV * inner, 1)
        part = part.astype(BF16)
        for o in range(2):
            doppler[2, :, 2 * channel + o] = part[o * M : (o + 1) * M].reshape(BLOCKS, GROUP, RA)


def correct(g, half, matrix, doppler, bands, phase, place, merge, merged):
    low = doppler[half, g].reshape(M, RA)
    if half:
        both = dot(matrix[g], jnp.concatenate([low, doppler[2, g].reshape(M, RA)], axis=1))
        near, far = both[:, :RA], both[:, RA:]
    else:
        near = dot(matrix[g], low)
    rows = []
    for j in range(CH):
        spot = place[half, g, j]
        here = spot < RA
        spot = spot & (RA - 1)
        before = place[0, g, j] & (RA - 1)
        pair = []
        for part in (2 * j, 2 * j + 1):
            at = slice(part * GROUP, (part + 1) * GROUP)
            if half:
                other = jnp.take_along_axis(far[at], spot, axis=1)
                bands[g, at, :] = jnp.take_along_axis(near[at], before, axis=1)
            else:
                other = bands[g, at, :]
            pair.append(jnp.where(here, jnp.take_along_axis(near[at], spot, axis=1), other))
        real, imag = scaled(*pair, phase[half, g, 2 * j], phase[half, g, 2 * j + 1])
        rows += [real.astype(BF16), imag.astype(BF16)]
    mixed = dot(merge[...], jnp.concatenate(rows, axis=0)).astype(BF16)
    merged[:, :, g] = mixed.reshape(CH, 2, GROUP, RA)


def invert(q, inverse, merged, image):
    part = dot(inverse[q], merged[q].reshape(2 * M, RA))
    for o in range(2):
        image[pl.ds(o * CH * RA + q, RA, stride=CH), :] = part[o * RA : (o + 1) * RA]


def focus_kernel(
    x_hbm,
    replica_hbm,
    w1_hbm,
    v2_hbm,
    v3_hbm,
    twiddle_hbm,
    w4_hbm,
    bank_hbm,
    spread_hbm,
    rate_hbm,
    width_hbm,
    migration_hbm,
    forward_hbm,
    merge_hbm,
    inverse_hbm,
    out_hbm,
    x,
    replica,
    w1,
    v2,
    v3,
    twiddle,
    w4,
    bank,
    spread,
    rate,
    width,
    migration,
    forward,
    merge,
    inverse,
    natural,
    spectrum,
    turn,
    rim,
    sent,
    held,
    matrix,
    doppler,
    bands,
    phase,
    place,
    merged,
    image,
    result,
    x_sem,
    table_sem,
    far_send,
    far_recv,
    near_send,
    near_recv,
    own_sem,
    out_sem,
):
    block = lax.axis_index("az")
    me = lax.axis_index("rg")
    px, pz, core = me // 8, (me // 2) % 4, me % 2
    above, below = (block + 1) % N_AZ, (block + N_AZ - 1) % N_AZ

    peers = [
        (px + x) % 4 * 8 + (pz + z) % 4 * 2 + (core + c) % 2
        for x, z in FAR_FIRST
        for c in range(2)
        if (x, z, c) != (0, 0, 0)
    ]

    fetches = [
        pltpu.make_async_copy(x_hbm.at[:, pl.ds(2 * n, 2)], x.at[:, pl.ds(2 * n, 2)], x_sem.at[n])
        for n in range(4)
    ]
    sources = [replica_hbm, w1_hbm, v2_hbm, v3_hbm, twiddle_hbm, w4_hbm, bank_hbm, spread_hbm]
    sources += [rate_hbm, width_hbm, migration_hbm, forward_hbm, merge_hbm, inverse_hbm]
    targets = [replica, w1, v2, v3, twiddle, w4, bank, spread]
    targets += [rate, width, migration, forward, merge, inverse]
    tables = [
        pltpu.make_async_copy(source, target, table_sem.at[n])
        for n, (source, target) in enumerate(zip(sources, targets))
    ]
    for copy in fetches[:1] + tables[:6] + fetches[1:] + tables[6:]:
        copy.start()

    barrier = pltpu.get_barrier_semaphore()

    for target in peers:
        pl.semaphore_signal(barrier, inc=1, device_id=(block, target), device_id_type=MESH)

    for other in (above, below):
        pl.semaphore_signal(barrier, inc=1, device_id=(other, me), device_id_type=MESH)

    own = [
        pltpu.make_async_copy(
            sent.at[me, pl.ds(low, high - low)],
            held.at[16 + me, pl.ds(low, high - low)],
            own_sem.at[n],
        )
        for n, (low, high) in enumerate(CUTS)
    ]

    def send(n):
        low, high = CUTS[n]
        units = pl.ds(low, high - low)

        for target in peers:
            pltpu.make_async_remote_copy(
                src_ref=sent.at[target, units],
                dst_ref=held.at[16 + me, units],
                send_sem=far_send.at[n],
                recv_sem=far_recv.at[n],
                device_id=(block, target),
                device_id_type=MESH,
            ).start()

        own[n].start()

    def onward(n, up):
        low, high = CUTS[n]
        units = pl.ds(low, high - low)
        return pltpu.make_async_remote_copy(
            src_ref=held.at[pl.ds(32 if up else 16, 16), units],
            dst_ref=held.at[pl.ds(0 if up else 48, 16), units],
            send_sem=near_send.at[int(up), n],
            recv_sem=near_recv.at[int(up), n],
            device_id=(above if up else below, me),
            device_id_type=MESH,
        )

    def relay(n):
        low, high = CUTS[n]
        whole = held.at[pl.ds(16, N_RG - 1), pl.ds(low, high - low)]
        pltpu.make_async_copy(whole, whole, far_recv.at[n]).wait()
        own[n].wait()

        @pl.when(block < N_AZ - 1)
        def _():
            onward(n, True).start()

        @pl.when(block > 0)
        def _():
            onward(n, False).start()

    def arrive(n):
        @pl.when(block < N_AZ - 1)
        def _():
            onward(n, False).wait_recv()

        @pl.when(block > 0)
        def _():
            onward(n, True).wait_recv()

    tables[0].wait()
    load_spectrum(replica, natural, spectrum)
    small = (w1, v2, v3, w4, twiddle)
    for n in range(4):
        fetches[n].wait()
        if n == 0:
            for copy in tables[1:6]:
                copy.wait()
        compress_pair(2 * n, n % 2, x, small, spectrum, turn, rim, sent)
        if n == 0:
            pl.semaphore_wait(barrier, N_RG + 1)
        send(n)
    for chunk in range(4, len(CUTS)):
        send(chunk)

    @pl.when(block == 0)
    def _():
        held[0:16] = jnp.zeros((16, UNITS, 8, RA), BF16)

    @pl.when(block == N_AZ - 1)
    def _():
        held[48:64] = jnp.zeros((16, UNITS, 8, RA), BF16)

    def phases(half, low, high):
        @pl.loop(low, high)
        def _(g):
            build_phases(g, half, rate, width, migration, phase, place)

    writes = [
        pltpu.make_async_copy(
            result.at[half, o],
            out_hbm.at[o, :, pl.ds(half * RA, RA)],
            out_sem.at[2 * half + o],
        )
        for half in range(2)
        for o in range(2)
    ]

    def complete(half, start=0):
        for g in range(start, BLOCKS):
            correct(g, half, matrix, doppler, bands, phase, place, merge, merged)
        for q in range(CH):
            invert(q, inverse, merged, image)

        for o in range(2):
            result[half, o] = image[o * CH * RA : (o + 1) * CH * RA, :].astype(BF16)
            writes[2 * half + o].start()

    def forward_chunk(n):
        arrive(n)
        if n == 4:
            forward_edges(held, forward, doppler)
        else:
            forward_pair(2 * (n % 5), int(n < 4), held, forward, doppler)

    relay(0)
    for copy in tables[6:11]:
        copy.wait()
    build_matrix(bank, spread, matrix)
    relay(1)
    phases(1, 0, 8)
    relay(2)
    phases(1, 8, 16)
    relay(3)
    phases(0, 0, 8)
    relay(4)
    phases(0, 8, 16)
    for copy in tables[11:]:
        copy.wait()
    relay(5)
    forward_chunk(0)
    forward_chunk(1)
    relay(6)
    forward_chunk(2)
    forward_chunk(3)
    relay(7)
    forward_chunk(4)
    for g in range(6):
        correct(g, 1, matrix, doppler, bands, phase, place, merge, merged)
    relay(8)
    complete(1, 6)
    for n in range(5, len(CUTS)):
        forward_chunk(n)
    complete(0)

    for n, (low, high) in enumerate(CUTS):
        whole = held.at[pl.ds(16, N_RG - 1), pl.ds(low, high - low)]
        pltpu.make_async_copy(whole, whole, far_send.at[n]).wait()

        @pl.when(block < N_AZ - 1)
        def _():
            onward(n, True).wait_send()

        @pl.when(block > 0)
        def _():
            onward(n, False).wait_send()

    for copy in writes:
        copy.wait()


def shards(echoes, replica, filter_bank, doppler_rate, doppler_width, migration):
    w1, v2, v3, w4, twiddle = range_tables()
    forward, inverse, merge, spread = azimuth_tables()
    operands = [echoes, replica]
    operands += [jnp.asarray(t) for t in (w1, v2, v3, twiddle, w4)]
    operands += [filter_bank.reshape(2 * CH * CH, M), jnp.asarray(spread)]
    operands += [a.reshape(1, 2 * RA) for a in (doppler_rate, doppler_width, migration)]
    operands += [jnp.asarray(t) for t in (forward, merge, inverse)]
    hbm = pl.BlockSpec(memory_space=pl.ANY)
    count = len(CUTS)
    return pl.pallas_call(
        focus_kernel,
        out_shape=jax.ShapeDtypeStruct((2, CH * RA, 2 * RA), BF16),
        in_specs=[hbm] * 15,
        out_specs=hbm,
        scratch_shapes=[
            pltpu.VMEM((2, CH, 4, R), BF16),
            *[pltpu.VMEM(o.shape, o.dtype) for o in operands[1:]],
            pltpu.VMEM((2 * RB, RA), F32),
            pltpu.VMEM((2, RB, RA), F32),
            pltpu.VMEM((2, 2, 4 * RB, RA), F32),
            pltpu.VMEM((N_RG * 8, RA), F32),
            pltpu.VMEM((N_RG, UNITS, 8, RA), BF16),
            pltpu.VMEM((2 * N_RG, UNITS, 8, RA), BF16),
            pltpu.VMEM((BLOCKS, M, M), BF16),
            pltpu.VMEM((3, BLOCKS, 2 * CH, GROUP, RA), BF16),
            pltpu.VMEM((BLOCKS, M, RA), F32),
            pltpu.VMEM((2, BLOCKS, 2 * CH, GROUP, RA), F32),
            pltpu.VMEM((2, BLOCKS, CH, GROUP, RA), jnp.int32),
            pltpu.VMEM((CH, 2, BLOCKS, GROUP, RA), BF16),
            pltpu.VMEM((2 * CH * RA, RA), F32),
            pltpu.VMEM((2, 2, CH * RA, RA), BF16),
            pltpu.SemaphoreType.DMA((4,)),
            pltpu.SemaphoreType.DMA((14,)),
            pltpu.SemaphoreType.DMA((count,)),
            pltpu.SemaphoreType.DMA((count,)),
            pltpu.SemaphoreType.DMA((2, count)),
            pltpu.SemaphoreType.DMA((2, count)),
            pltpu.SemaphoreType.DMA((count,)),
            pltpu.SemaphoreType.DMA((4,)),
        ],
        compiler_params=pltpu.CompilerParams(
            collective_id=0, has_side_effects=True, vmem_limit_bytes=60 * 2**20
        ),
        cost_estimate=pl.CostEstimate(
            flops=2 * 2_000_000_000, bytes_accessed=2**23, transcendentals=0
        ),
        name="focus",
    )(*operands)


def solution(mesh):
    placed = (P(None, None, ("az", "rg"), None), P(), P(), P("rg"), P("rg"), P("rg"))
    return jax.shard_map(
        shards, mesh=mesh, in_specs=placed, out_specs=P(None, "az", "rg"), check_vma=False
    )
```

```python
import functools
import math

import jax
import jax.numpy as jnp
import ml_dtypes
import numpy as np
from jax import lax
from jax.experimental import pallas as pl
from jax.experimental.pallas import tpu as pltpu
from jax.sharding import PartitionSpec as P

CH = 8
RA = 128
RB = 64
R = RA * RB
M = 256
E = 64
OV = 32
N_AZ = 4
N_RG = 32
GROUP = 16
BLOCKS = M // GROUP
UNITS = 18
CUTS = tuple((n, n + 2) for n in range(0, UNITS, 2))
FAR_FIRST = ((2, 2), (1, 2), (2, 1), (3, 2), (2, 3), (1, 1), (3, 3), (1, 3), (3, 1))
FAR_FIRST += ((2, 0), (0, 2), (1, 0), (0, 1), (3, 0), (0, 3), (0, 0))
MESH = pl.DeviceIdType.MESH
F32 = jnp.float32
BF16 = jnp.bfloat16


def stored(table):
    return np.asarray(table, np.float32).astype(ml_dtypes.bfloat16)


def angle_pair(product, length):
    angles = 2.0 * math.pi / length * (np.asarray(product) % length)
    return np.cos(angles), np.sin(angles)


def real_rows(cosine, sine):
    return np.stack(
        [np.stack([cosine, -sine], axis=1), np.stack([sine, cosine], axis=1)]
    )


def unit_of(channel, half):
    return channel if half else 10 + channel


def edge_unit(group):
    return CH + group


def range_tables():
    ids = np.arange(RB)
    cosine, sine = angle_pair(ids[:, None] * ids[None, :], RB)
    w1 = real_rows(cosine, -sine).reshape(2 * RB, 2 * RB)
    w4 = real_rows(cosine, sine) / R
    w4 = np.einsum("obik,pn->bopink", w4, np.eye(4)).reshape(8 * RB, 8 * RB)
    ids = np.arange(RA)
    order = 2 * (ids % RB) + ids // RB
    cosine, sine = angle_pair(ids[:, None] * ids[None, :], RA)
    v2 = real_rows(cosine, -sine)[:, order].reshape(2 * RA, 2 * RA).T
    v3 = real_rows(cosine, sine)[..., order].reshape(2 * RA, 2 * RA).T
    cosine, sine = angle_pair(np.arange(RB)[:, None] * np.arange(RA)[None, :], R)
    twiddle = np.stack([cosine, sine]).astype(np.float32)
    return stored(w1), stored(v2), stored(v3), stored(w4), twiddle


def azimuth_tables():
    freqs = np.arange(M)
    cosine, sine = angle_pair(freqs[:, None] * np.arange(M)[None, :], M)
    forward = real_rows(cosine, -sine)
    forward = forward.reshape(2, M, 2, M // 4, 4).transpose(0, 1, 3, 2, 4).reshape(2 * M, 2 * M)
    slots = np.arange(E, M - E)
    inverse = []
    for q in range(CH):
        cosine, sine = angle_pair((CH * slots[:, None] + q) * freqs[None, :], CH * M)
        inverse.append(real_rows(cosine, sine).reshape(M, 2 * M) / (CH * M))
    ids = np.arange(CH)
    cosine, sine = angle_pair(ids[:, None] * ids[None, :], CH)
    merge = real_rows(cosine, sine).transpose(1, 0, 2, 3)
    merge = merge.transpose(0, 1, 3, 2).reshape(2 * CH, 2 * CH)
    merge = np.kron(merge, np.eye(GROUP))
    spread = np.zeros((2, CH, CH, CH, 2, CH, 2, GROUP))
    for j in range(CH):
        for c in range(CH):
            spread[0, j, c, j, 0, c, 0] = 1.0
            spread[1, j, c, j, 0, c, 1] = -1.0
            spread[1, j, c, j, 1, c, 0] = 1.0
            spread[0, j, c, j, 1, c, 1] = 1.0
    spread = spread.reshape(2 * CH * CH, 2 * CH * 2 * CH * GROUP)
    return stored(forward), stored(np.stack(inverse)), stored(merge), stored(spread)


def dot(a, b):
    return jnp.dot(a, b, preferred_element_type=F32)


def scaled(real, imag, table_real, table_imag):
    return (
        real * table_real - imag * table_imag,
        real * table_imag + imag * table_real,
    )


def load_spectrum(replica, natural, spectrum):
    values = replica[...]
    for n in range(RB):
        natural[pl.ds(n, 2, stride=RB), :] = values[:, n * RA : (n + 1) * RA]
    turned = natural[...].T
    for i in range(2):
        part = turned[:, i * RB : (i + 1) * RB]
        spectrum[i] = jnp.concatenate([part[:RB], part[RB:]], axis=1)


def compress_pair(first_channel, inner, x, tables, spectrum, turn, rim, sent):
    w1, v2, v3, w4, twiddle = tables
    results = []
    for c in range(2):
        channel = first_channel + c
        for i in range(2):
            values = x[i, channel].astype(F32)
            for n in range(RB):
                turn[c, i, pl.ds(n, 4, stride=RB), :] = values[:, n * RA : (n + 1) * RA]
        columns = [
            jnp.concatenate(
                [turn[c, i, p * RB : (p + 1) * RB, :] for i in range(2)], axis=0
            ).astype(BF16)
            for p in range(4)
        ]
        current = dot(w1[...], jnp.concatenate(columns, axis=1))
        rows = []
        for p in range(4):
            part = current[:, p * RA : (p + 1) * RA]
            pair = scaled(part[:RB], part[RB:], twiddle[0], -twiddle[1])
            rows.append(jnp.concatenate(pair, axis=1).astype(BF16))
        current = dot(jnp.concatenate(rows, axis=0), v2[...])
        rows = []
        for p in range(4):
            part = current[p * RB : (p + 1) * RB]
            pair = scaled(part[:, :RA], part[:, RA:], spectrum[0], spectrum[1])
            rows.append(jnp.concatenate(pair, axis=1).astype(BF16))
        current = dot(jnp.concatenate(rows, axis=0), v3[...])
        parts = []
        for p in range(4):
            part = current[p * RB : (p + 1) * RB]
            parts.append(scaled(part[:, :RA], part[:, RA:], twiddle[0], twiddle[1]))
        results.append(
            jnp.concatenate([parts[p][i] for i in range(2) for p in range(4)], axis=0).astype(BF16)
        )
    current = dot(w4[...], jnp.concatenate(results, axis=1))
    lane_group = lax.broadcasted_iota(jnp.int32, (N_RG * 8, RA), 1) // OV
    edge = rim[...] if inner else None
    for c in range(2):
        turned = current[:, c * RA : (c + 1) * RA].reshape(N_RG, 2, 8, RA)
        for half in range(2):
            sent[:, unit_of(first_channel + c, half)] = turned[:, half].astype(BF16)
        low = turned[:, 0].reshape(N_RG * 8, RA)
        spot = 2 * inner + c
        if spot:
            edge = jnp.where(lane_group == spot, pltpu.roll(low, OV * spot, 1), edge)
        else:
            edge = low
    if not inner:
        rim[...] = edge
        return
    unit = edge_unit(first_channel // 4)
    kept = edge.astype(BF16).reshape(N_RG, 8, RA)
    sent[0 : N_RG - 1, unit] = kept[1:]
    sent[N_RG - 1, unit] = jnp.zeros((8, RA), BF16)


def sine_cosine(angle):
    turns = angle * (2.0 / math.pi)
    quarter = (turns + 0.5).astype(jnp.int32)
    rest = (turns - quarter.astype(F32)) * (0.5 * math.pi)
    square = rest * rest
    sine = -1.9515295891e-4 * square + 8.3321608736e-3
    sine = sine * square - 1.6666654611e-1
    sine = sine * square * rest + rest
    cosine = 2.443315711809948e-5 * square - 1.388731625493765e-3
    cosine = cosine * square + 4.166664568298827e-2
    cosine = cosine * square * square - 0.5 * square + 1.0
    swap = (quarter & 1) == 1
    real = jnp.where(swap, sine, cosine)
    imag = jnp.where(swap, cosine, sine)
    real = jnp.where(((quarter + 1) & 2) == 2, -real, real)
    imag = jnp.where((quarter & 2) == 2, -imag, imag)
    return real, imag


def build_matrix(bank, spread, matrix):
    same = (
        lax.broadcasted_iota(jnp.int32, (M, M), 0) % GROUP
        == lax.broadcasted_iota(jnp.int32, (M, M), 1) % GROUP
    )
    for n in range(2 * CH):
        wide = lax.dot_general(
            bank[...],
            spread[:, n * M : (n + 1) * M],
            (((0,), (0,)), ((), ())),
            preferred_element_type=F32,
        )
        wide = jnp.where(same, wide, 0.0).astype(BF16)
        matrix[:, n * GROUP : (n + 1) * GROUP, :] = wide.reshape(BLOCKS, GROUP, M)


def build_phases(g, half, rate, width, migration, phase, place):
    cols = slice(half * RA, (half + 1) * RA)
    row = lax.broadcasted_iota(jnp.int32, (GROUP, RA), 0)
    lane = lax.broadcasted_iota(jnp.int32, (GROUP, RA), 1)
    row = (row + g * GROUP).astype(F32)
    scale = 2.0 / (CH * M)
    per_level = jnp.broadcast_to(migration[:, cols].astype(F32) * scale, (GROUP, RA))
    rates = jnp.broadcast_to(rate[:, cols], (GROUP, RA))
    widths = jnp.broadcast_to(width[:, cols].astype(F32), (GROUP, RA))
    for j in range(CH):
        centered = row + float(j * M if j < CH // 2 else j * M - CH * M)
        square = centered * centered
        offsets = (per_level * jnp.floor(square * scale)).astype(jnp.int32)
        place[half, g, j] = lane + offsets
        real, imag = sine_cosine(rates * (square * (1.0 / (CH * M) ** 2)))
        inside = jnp.abs(centered) < widths
        phase[half, g, 2 * j] = jnp.where(inside, real, 0.0)
        phase[half, g, 2 * j + 1] = jnp.where(inside, imag, 0.0)


def gathered(held, unit):
    return held[:, unit].astype(F32).reshape(2 * M, RA).astype(BF16)


def forward_pair(channel, half, held, forward, doppler):
    units = [unit_of(channel + n, half) for n in range(2)]
    pulses = jnp.concatenate([gathered(held, unit) for unit in units], axis=1)
    bins = dot(forward[...], pulses).astype(BF16)
    for n in range(2):
        for o in range(2):
            doppler[half, :, 2 * (channel + n) + o] = bins[
                o * M : (o + 1) * M, n * RA : (n + 1) * RA
            ].reshape(BLOCKS, GROUP, RA)


def forward_edges(held, forward, doppler):
    pulses = jnp.concatenate([gathered(held, edge_unit(n)) for n in range(2)], axis=1)
    bins = dot(forward[...], pulses)
    for channel in range(CH):
        group, inner = channel // 4, channel % 4
        part = bins[:, group * RA : (group + 1) * RA]
        if inner:
            part = pltpu.roll(part, RA - OV * inner, 1)
        part = part.astype(BF16)
        for o in range(2):
            doppler[2, :, 2 * channel + o] = part[o * M : (o + 1) * M].reshape(BLOCKS, GROUP, RA)


def slide(near, far, offsets, lane):
    one = pltpu.roll(jnp.where(lane < 1, far, near), RA - 1, 1)
    two = pltpu.roll(jnp.where(lane < 2, far, near), RA - 2, 1)
    return jnp.where(offsets == 0, near, jnp.where(offsets == 1, one, two))


def correct(g, half, matrix, doppler, bands, phase, place, merge, merged):
    lane = lax.broadcasted_iota(jnp.int32, (GROUP, RA), 1)
    low = doppler[half, g].reshape(M, RA)
    if half:
        both = dot(matrix[g], jnp.concatenate([low, doppler[2, g].reshape(M, RA)], axis=1))
        near, far = both[:, :RA], both[:, RA:]
    else:
        near = dot(matrix[g], low)
    rows = []
    for j in range(CH):
        spot = place[half, g, j]
        offsets = spot - lane
        here = spot < RA
        spot = spot & (RA - 1)
        before = place[0, g, j] & (RA - 1)
        pair = []
        for part in (2 * j, 2 * j + 1):
            at = slice(part * GROUP, (part + 1) * GROUP)
            if j in (0, CH - 1):
                pair.append(slide(near[at], far[at] if half else bands[g, at, :], offsets, lane))
                if half:
                    bands[g, at, :] = near[at]
                continue
            if half:
                other = jnp.take_along_axis(far[at], spot, axis=1)
                bands[g, at, :] = jnp.take_along_axis(near[at], before, axis=1)
            else:
                other = bands[g, at, :]
            pair.append(jnp.where(here, jnp.take_along_axis(near[at], spot, axis=1), other))
        real, imag = scaled(*pair, phase[half, g, 2 * j], phase[half, g, 2 * j + 1])
        rows += [real.astype(BF16), imag.astype(BF16)]
    mixed = dot(merge[...], jnp.concatenate(rows, axis=0)).astype(BF16)
    merged[:, :, g] = mixed.reshape(CH, 2, GROUP, RA)


def invert(q, inverse, merged, image):
    part = dot(inverse[q], merged[q].reshape(2 * M, RA))
    for o in range(2):
        image[pl.ds(o * CH * RA + q, RA, stride=CH), :] = part[o * RA : (o + 1) * RA]


def focus_kernel(
    x_hbm,
    replica_hbm,
    w1_hbm,
    v2_hbm,
    v3_hbm,
    twiddle_hbm,
    w4_hbm,
    bank_hbm,
    spread_hbm,
    rate_hbm,
    width_hbm,
    migration_hbm,
    forward_hbm,
    merge_hbm,
    inverse_hbm,
    out_hbm,
    x,
    replica,
    w1,
    v2,
    v3,
    twiddle,
    w4,
    bank,
    spread,
    rate,
    width,
    migration,
    forward,
    merge,
    inverse,
    natural,
    spectrum,
    turn,
    rim,
    sent,
    held,
    matrix,
    doppler,
    bands,
    phase,
    place,
    merged,
    image,
    result,
    x_sem,
    table_sem,
    far_send,
    far_recv,
    near_send,
    near_recv,
    own_sem,
    out_sem,
):
    block = lax.axis_index("az")
    me = lax.axis_index("rg")
    px, pz, core = me // 8, (me // 2) % 4, me % 2
    above, below = (block + 1) % N_AZ, (block + N_AZ - 1) % N_AZ

    peers = [
        (px + x) % 4 * 8 + (pz + z) % 4 * 2 + (core + c) % 2
        for x, z in FAR_FIRST
        for c in range(2)
        if (x, z, c) != (0, 0, 0)
    ]

    fetches = [
        pltpu.make_async_copy(x_hbm.at[:, pl.ds(2 * n, 2)], x.at[:, pl.ds(2 * n, 2)], x_sem.at[n])
        for n in range(4)
    ]
    sources = [replica_hbm, w1_hbm, v2_hbm, v3_hbm, twiddle_hbm, w4_hbm, bank_hbm, spread_hbm]
    sources += [rate_hbm, width_hbm, migration_hbm, forward_hbm, merge_hbm, inverse_hbm]
    targets = [replica, w1, v2, v3, twiddle, w4, bank, spread]
    targets += [rate, width, migration, forward, merge, inverse]
    tables = [
        pltpu.make_async_copy(source, target, table_sem.at[n])
        for n, (source, target) in enumerate(zip(sources, targets))
    ]
    for copy in fetches[:1] + tables[:6] + fetches[1:] + tables[6:]:
        copy.start()

    barrier = pltpu.get_barrier_semaphore()

    for target in peers:
        pl.semaphore_signal(barrier, inc=1, device_id=(block, target), device_id_type=MESH)

    for other in (above, below):
        pl.semaphore_signal(barrier, inc=1, device_id=(other, me), device_id_type=MESH)

    own = [
        pltpu.make_async_copy(
            sent.at[me, pl.ds(low, high - low)],
            held.at[16 + me, pl.ds(low, high - low)],
            own_sem.at[n],
        )
        for n, (low, high) in enumerate(CUTS)
    ]

    def send(n):
        low, high = CUTS[n]
        units = pl.ds(low, high - low)

        for target in peers:
            pltpu.make_async_remote_copy(
                src_ref=sent.at[target, units],
                dst_ref=held.at[16 + me, units],
                send_sem=far_send.at[n],
                recv_sem=far_recv.at[n],
                device_id=(block, target),
                device_id_type=MESH,
            ).start()

        own[n].start()

    def onward(n, up):
        low, high = CUTS[n]
        units = pl.ds(low, high - low)
        return pltpu.make_async_remote_copy(
            src_ref=held.at[pl.ds(32 if up else 16, 16), units],
            dst_ref=held.at[pl.ds(0 if up else 48, 16), units],
            send_sem=near_send.at[int(up), n],
            recv_sem=near_recv.at[int(up), n],
            device_id=(above if up else below, me),
            device_id_type=MESH,
        )

    def relay(n):
        low, high = CUTS[n]
        whole = held.at[pl.ds(16, N_RG - 1), pl.ds(low, high - low)]
        pltpu.make_async_copy(whole, whole, far_recv.at[n]).wait()
        own[n].wait()

        @pl.when(block < N_AZ - 1)
        def _():
            onward(n, True).start()

        @pl.when(block > 0)
        def _():
            onward(n, False).start()

    def arrive(n):
        @pl.when(block < N_AZ - 1)
        def _():
            onward(n, False).wait_recv()

        @pl.when(block > 0)
        def _():
            onward(n, True).wait_recv()

    tables[0].wait()
    load_spectrum(replica, natural, spectrum)
    small = (w1, v2, v3, w4, twiddle)
    for n in range(4):
        fetches[n].wait()
        if n == 0:
            for copy in tables[1:6]:
                copy.wait()
        compress_pair(2 * n, n % 2, x, small, spectrum, turn, rim, sent)
        if n == 0:
            pl.semaphore_wait(barrier, N_RG + 1)
        send(n)
    for chunk in range(4, len(CUTS)):
        send(chunk)

    @pl.when(block == 0)
    def _():
        held[0:16] = jnp.zeros((16, UNITS, 8, RA), BF16)

    @pl.when(block == N_AZ - 1)
    def _():
        held[48:64] = jnp.zeros((16, UNITS, 8, RA), BF16)

    def phases(half, low, high):
        @pl.loop(low, high)
        def _(g):
            build_phases(g, half, rate, width, migration, phase, place)

    writes = [
        pltpu.make_async_copy(
            result.at[half, o],
            out_hbm.at[o, :, pl.ds(half * RA, RA)],
            out_sem.at[2 * half + o],
        )
        for half in range(2)
        for o in range(2)
    ]

    def complete(half, start=0):
        for g in range(start, BLOCKS):
            correct(g, half, matrix, doppler, bands, phase, place, merge, merged)
        for q in range(CH):
            invert(q, inverse, merged, image)

        for o in range(2):
            result[half, o] = image[o * CH * RA : (o + 1) * CH * RA, :].astype(BF16)
            writes[2 * half + o].start()

    def forward_chunk(n):
        arrive(n)
        if n == 4:
            forward_edges(held, forward, doppler)
        else:
            forward_pair(2 * (n % 5), int(n < 4), held, forward, doppler)

    relay(0)
    for copy in tables[6:11]:
        copy.wait()
    build_matrix(bank, spread, matrix)
    relay(1)
    phases(1, 0, 8)
    relay(2)
    phases(1, 8, 16)
    relay(3)
    phases(0, 0, 8)
    relay(4)
    phases(0, 8, 16)
    for copy in tables[11:]:
        copy.wait()
    relay(5)
    forward_chunk(0)
    forward_chunk(1)
    relay(6)
    forward_chunk(2)
    forward_chunk(3)
    relay(7)
    forward_chunk(4)
    for g in range(6):
        correct(g, 1, matrix, doppler, bands, phase, place, merge, merged)
    relay(8)
    complete(1, 6)
    for n in range(5, len(CUTS)):
        forward_chunk(n)
    complete(0)

    for n, (low, high) in enumerate(CUTS):
        whole = held.at[pl.ds(16, N_RG - 1), pl.ds(low, high - low)]
        pltpu.make_async_copy(whole, whole, far_send.at[n]).wait()

        @pl.when(block < N_AZ - 1)
        def _():
            onward(n, True).wait_send()

        @pl.when(block > 0)
        def _():
            onward(n, False).wait_send()

    for copy in writes:
        copy.wait()


def shards(echoes, replica, filter_bank, doppler_rate, doppler_width, migration):
    w1, v2, v3, w4, twiddle = range_tables()
    forward, inverse, merge, spread = azimuth_tables()
    operands = [echoes, replica]
    operands += [jnp.asarray(t) for t in (w1, v2, v3, twiddle, w4)]
    operands += [filter_bank.reshape(2 * CH * CH, M), jnp.asarray(spread)]
    operands += [a.reshape(1, 2 * RA) for a in (doppler_rate, doppler_width, migration)]
    operands += [jnp.asarray(t) for t in (forward, merge, inverse)]
    hbm = pl.BlockSpec(memory_space=pl.ANY)
    count = len(CUTS)
    return pl.pallas_call(
        focus_kernel,
        out_shape=jax.ShapeDtypeStruct((2, CH * RA, 2 * RA), BF16),
        in_specs=[hbm] * 15,
        out_specs=hbm,
        scratch_shapes=[
            pltpu.VMEM((2, CH, 4, R), BF16),
            *[pltpu.VMEM(o.shape, o.dtype) for o in operands[1:]],
            pltpu.VMEM((2 * RB, RA), F32),
            pltpu.VMEM((2, RB, RA), F32),
            pltpu.VMEM((2, 2, 4 * RB, RA), F32),
            pltpu.VMEM((N_RG * 8, RA), F32),
            pltpu.VMEM((N_RG, UNITS, 8, RA), BF16),
            pltpu.VMEM((2 * N_RG, UNITS, 8, RA), BF16),
            pltpu.VMEM((BLOCKS, M, M), BF16),
            pltpu.VMEM((3, BLOCKS, 2 * CH, GROUP, RA), BF16),
            pltpu.VMEM((BLOCKS, M, RA), F32),
            pltpu.VMEM((2, BLOCKS, 2 * CH, GROUP, RA), F32),
            pltpu.VMEM((2, BLOCKS, CH, GROUP, RA), jnp.int32),
            pltpu.VMEM((CH, 2, BLOCKS, GROUP, RA), BF16),
            pltpu.VMEM((2 * CH * RA, RA), F32),
            pltpu.VMEM((2, 2, CH * RA, RA), BF16),
            pltpu.SemaphoreType.DMA((4,)),
            pltpu.SemaphoreType.DMA((14,)),
            pltpu.SemaphoreType.DMA((count,)),
            pltpu.SemaphoreType.DMA((count,)),
            pltpu.SemaphoreType.DMA((2, count)),
            pltpu.SemaphoreType.DMA((2, count)),
            pltpu.SemaphoreType.DMA((count,)),
            pltpu.SemaphoreType.DMA((4,)),
        ],
        compiler_params=pltpu.CompilerParams(
            collective_id=0, has_side_effects=True, vmem_limit_bytes=60 * 2**20
        ),
        cost_estimate=pl.CostEstimate(
            flops=2 * 2_000_000_000, bytes_accessed=2**23, transcendentals=0
        ),
        name="focus",
    )(*operands)


def solution(mesh):
    placed = (P(None, None, ("az", "rg"), None), P(), P(), P("rg"), P("rg"), P("rg"))
    return jax.shard_map(
        shards, mesh=mesh, in_specs=placed, out_specs=P(None, "az", "rg"), check_vma=False
    )
```

```python
import functools
import math

import jax
import jax.numpy as jnp
import ml_dtypes
import numpy as np
from jax import lax
from jax.experimental import pallas as pl
from jax.experimental.pallas import tpu as pltpu
from jax.sharding import PartitionSpec as P

CH = 8
RA = 128
RB = 64
R = RA * RB
M = 256
E = 64
OV = 32
N_AZ = 4
N_RG = 32
GROUP = 16
BLOCKS = M // GROUP
UNITS = 18
CUTS = tuple((n, n + 2) for n in range(0, UNITS, 2))
FAR_FIRST = ((2, 2), (1, 2), (2, 1), (3, 2), (2, 3), (1, 1), (3, 3), (1, 3), (3, 1))
FAR_FIRST += ((2, 0), (0, 2), (1, 0), (0, 1), (3, 0), (0, 3), (0, 0))
MESH = pl.DeviceIdType.MESH
F32 = jnp.float32
BF16 = jnp.bfloat16


def stored(table):
    return np.asarray(table, np.float32).astype(ml_dtypes.bfloat16)


def angle_pair(product, length):
    angles = 2.0 * math.pi / length * (np.asarray(product) % length)
    return np.cos(angles), np.sin(angles)


def real_rows(cosine, sine):
    return np.stack(
        [np.stack([cosine, -sine], axis=1), np.stack([sine, cosine], axis=1)]
    )


def unit_of(channel, half):
    return channel if half else 10 + channel


def edge_unit(group):
    return CH + group


def range_tables():
    ids = np.arange(RB)
    cosine, sine = angle_pair(ids[:, None] * ids[None, :], RB)
    w1 = real_rows(cosine, -sine).reshape(2 * RB, 2 * RB)
    w4 = real_rows(cosine, sine) / R
    w4 = np.einsum("obik,pn->bopink", w4, np.eye(4)).reshape(8 * RB, 8 * RB)
    ids = np.arange(RA)
    order = 2 * (ids % RB) + ids // RB
    cosine, sine = angle_pair(ids[:, None] * ids[None, :], RA)
    v2 = real_rows(cosine, -sine)[:, order].reshape(2 * RA, 2 * RA).T
    v3 = real_rows(cosine, sine)[..., order].reshape(2 * RA, 2 * RA).T
    cosine, sine = angle_pair(np.arange(RB)[:, None] * np.arange(RA)[None, :], R)
    twiddle = np.stack([cosine, sine]).astype(np.float32)
    return stored(w1), stored(v2), stored(v3), stored(w4), twiddle


def azimuth_tables():
    freqs = np.arange(M)
    cosine, sine = angle_pair(freqs[:, None] * np.arange(M)[None, :], M)
    forward = real_rows(cosine, -sine)
    forward = forward.reshape(2, M, 2, M // 4, 4).transpose(0, 1, 3, 2, 4).reshape(2 * M, 2 * M)
    slots = np.arange(E, M - E)
    inverse = []
    for q in range(CH):
        cosine, sine = angle_pair((CH * slots[:, None] + q) * freqs[None, :], CH * M)
        inverse.append(real_rows(cosine, sine).reshape(M, 2 * M) / (CH * M))
    ids = np.arange(CH)
    cosine, sine = angle_pair(ids[:, None] * ids[None, :], CH)
    merge = real_rows(cosine, sine).transpose(1, 0, 2, 3)
    merge = merge.transpose(0, 1, 3, 2).reshape(2 * CH, 2 * CH)
    merge = np.kron(merge, np.eye(GROUP))
    spread = np.zeros((2, CH, CH, CH, 2, CH, 2, GROUP))
    for j in range(CH):
        for c in range(CH):
            spread[0, j, c, j, 0, c, 0] = 1.0
            spread[1, j, c, j, 0, c, 1] = -1.0
            spread[1, j, c, j, 1, c, 0] = 1.0
            spread[0, j, c, j, 1, c, 1] = 1.0
    spread = spread.reshape(2 * CH * CH, 2 * CH * 2 * CH * GROUP)
    return stored(forward), stored(np.stack(inverse)), stored(merge), stored(spread)


def dot(a, b):
    return jnp.dot(a, b, preferred_element_type=F32)


def scaled(real, imag, table_real, table_imag):
    return (
        real * table_real - imag * table_imag,
        real * table_imag + imag * table_real,
    )


def load_spectrum(replica, natural, spectrum):
    values = replica[...]
    for n in range(RB):
        natural[pl.ds(n, 2, stride=RB), :] = values[:, n * RA : (n + 1) * RA]
    turned = natural[...].T
    for i in range(2):
        part = turned[:, i * RB : (i + 1) * RB]
        spectrum[i] = jnp.concatenate([part[:RB], part[RB:]], axis=1)


def compress_pair(first_channel, inner, x, tables, spectrum, turn, rim, sent):
    w1, v2, v3, w4, twiddle = tables
    results = []
    for c in range(2):
        channel = first_channel + c
        for i in range(2):
            values = x[i, channel].astype(F32)
            for n in range(RB):
                turn[c, i, pl.ds(n, 4, stride=RB), :] = values[:, n * RA : (n + 1) * RA]
        columns = [
            jnp.concatenate(
                [turn[c, i, p * RB : (p + 1) * RB, :] for i in range(2)], axis=0
            ).astype(BF16)
            for p in range(4)
        ]
        current = dot(w1[...], jnp.concatenate(columns, axis=1))
        rows = []
        for p in range(4):
            part = current[:, p * RA : (p + 1) * RA]
            pair = scaled(part[:RB], part[RB:], twiddle[0], -twiddle[1])
            rows.append(jnp.concatenate(pair, axis=1).astype(BF16))
        current = dot(jnp.concatenate(rows, axis=0), v2[...])
        rows = []
        for p in range(4):
            part = current[p * RB : (p + 1) * RB]
            pair = scaled(part[:, :RA], part[:, RA:], spectrum[0], spectrum[1])
            rows.append(jnp.concatenate(pair, axis=1).astype(BF16))
        current = dot(jnp.concatenate(rows, axis=0), v3[...])
        parts = []
        for p in range(4):
            part = current[p * RB : (p + 1) * RB]
            parts.append(scaled(part[:, :RA], part[:, RA:], twiddle[0], twiddle[1]))
        results.append(
            jnp.concatenate([parts[p][i] for i in range(2) for p in range(4)], axis=0).astype(BF16)
        )
    current = dot(w4[...], jnp.concatenate(results, axis=1))
    lane_group = lax.broadcasted_iota(jnp.int32, (N_RG * 8, RA), 1) // OV
    edge = rim[...] if inner else None
    for c in range(2):
        turned = current[:, c * RA : (c + 1) * RA].reshape(N_RG, 2, 8, RA)
        for half in range(2):
            sent[:, unit_of(first_channel + c, half)] = turned[:, half].astype(BF16)
        low = turned[:, 0].reshape(N_RG * 8, RA)
        spot = 2 * inner + c
        if spot:
            edge = jnp.where(lane_group == spot, pltpu.roll(low, OV * spot, 1), edge)
        else:
            edge = low
    if not inner:
        rim[...] = edge
        return
    unit = edge_unit(first_channel // 4)
    kept = edge.astype(BF16).reshape(N_RG, 8, RA)
    sent[0 : N_RG - 1, unit] = kept[1:]
    sent[N_RG - 1, unit] = jnp.zeros((8, RA), BF16)


def sine_cosine(angle):
    turns = angle * (2.0 / math.pi)
    quarter = (turns + 0.5).astype(jnp.int32)
    rest = (turns - quarter.astype(F32)) * (0.5 * math.pi)
    square = rest * rest
    sine = -1.9515295891e-4 * square + 8.3321608736e-3
    sine = sine * square - 1.6666654611e-1
    sine = sine * square * rest + rest
    cosine = 2.443315711809948e-5 * square - 1.388731625493765e-3
    cosine = cosine * square + 4.166664568298827e-2
    cosine = cosine * square * square - 0.5 * square + 1.0
    swap = (quarter & 1) == 1
    real = jnp.where(swap, sine, cosine)
    imag = jnp.where(swap, cosine, sine)
    real = jnp.where(((quarter + 1) & 2) == 2, -real, real)
    imag = jnp.where((quarter & 2) == 2, -imag, imag)
    return real, imag


def build_matrix(bank, spread, matrix):
    same = (
        lax.broadcasted_iota(jnp.int32, (M, M), 0) % GROUP
        == lax.broadcasted_iota(jnp.int32, (M, M), 1) % GROUP
    )
    for n in range(2 * CH):
        wide = lax.dot_general(
            bank[...],
            spread[:, n * M : (n + 1) * M],
            (((0,), (0,)), ((), ())),
            preferred_element_type=F32,
        )
        wide = jnp.where(same, wide, 0.0).astype(BF16)
        matrix[:, n * GROUP : (n + 1) * GROUP, :] = wide.reshape(BLOCKS, GROUP, M)


def build_phases(g, half, rate, width, migration, phase, place):
    cols = slice(half * RA, (half + 1) * RA)
    row = lax.broadcasted_iota(jnp.int32, (GROUP, RA), 0)
    lane = lax.broadcasted_iota(jnp.int32, (GROUP, RA), 1)
    row = (row + g * GROUP).astype(F32)
    scale = 2.0 / (CH * M)
    per_level = jnp.broadcast_to(migration[:, cols].astype(F32) * scale, (GROUP, RA))
    rates = jnp.broadcast_to(rate[:, cols], (GROUP, RA))
    widths = jnp.broadcast_to(width[:, cols].astype(F32), (GROUP, RA))
    for j in range(CH):
        centered = row + float(j * M if j < CH // 2 else j * M - CH * M)
        square = centered * centered
        offsets = (per_level * jnp.floor(square * scale)).astype(jnp.int32)
        place[half, g, j] = lane + offsets
        real, imag = sine_cosine(rates * (square * (1.0 / (CH * M) ** 2)))
        inside = jnp.abs(centered) < widths
        phase[half, g, 2 * j] = jnp.where(inside, real, 0.0)
        phase[half, g, 2 * j + 1] = jnp.where(inside, imag, 0.0)


def gathered(held, unit):
    return held[:, unit].astype(F32).reshape(2 * M, RA).astype(BF16)


def forward_pair(channel, half, held, forward, doppler):
    units = [unit_of(channel + n, half) for n in range(2)]
    pulses = jnp.concatenate([gathered(held, unit) for unit in units], axis=1)
    bins = dot(forward[...], pulses).astype(BF16)
    for n in range(2):
        for o in range(2):
            doppler[half, :, 2 * (channel + n) + o] = bins[
                o * M : (o + 1) * M, n * RA : (n + 1) * RA
            ].reshape(BLOCKS, GROUP, RA)


def forward_edges(held, forward, doppler):
    pulses = jnp.concatenate([gathered(held, edge_unit(n)) for n in range(2)], axis=1)
    bins = dot(forward[...], pulses)
    for channel in range(CH):
        group, inner = channel // 4, channel % 4
        part = bins[:, group * RA : (group + 1) * RA]
        if inner:
            part = pltpu.roll(part, RA - OV * inner, 1)
        part = part.astype(BF16)
        for o in range(2):
            doppler[2, :, 2 * channel + o] = part[o * M : (o + 1) * M].reshape(BLOCKS, GROUP, RA)


def slide(near, far, offsets, lane):
    one = pltpu.roll(jnp.where(lane < 1, far, near), RA - 1, 1)
    two = pltpu.roll(jnp.where(lane < 2, far, near), RA - 2, 1)
    return jnp.where(offsets == 0, near, jnp.where(offsets == 1, one, two))


def correct(g, half, matrix, doppler, bands, phase, place, merge, merged):
    lane = lax.broadcasted_iota(jnp.int32, (GROUP, RA), 1)
    low = doppler[half, g].reshape(M, RA)
    if half:
        both = dot(matrix[g], jnp.concatenate([low, doppler[2, g].reshape(M, RA)], axis=1))
        near, far = both[:, :RA], both[:, RA:]
    else:
        near = dot(matrix[g], low)
    rows = []
    for j in range(CH):
        spot = place[half, g, j]
        offsets = spot - lane
        here = spot < RA
        spot = spot & (RA - 1)
        before = place[0, g, j] & (RA - 1)
        pair = []
        for part in (2 * j, 2 * j + 1):
            at = slice(part * GROUP, (part + 1) * GROUP)
            if j in (0, CH - 1):
                pair.append(slide(near[at], far[at] if half else bands[g, at, :], offsets, lane))
                if half:
                    bands[g, at, :] = near[at]
                continue
            if half:
                other = jnp.take_along_axis(far[at], spot, axis=1)
                bands[g, at, :] = jnp.take_along_axis(near[at], before, axis=1)
            else:
                other = bands[g, at, :]
            pair.append(jnp.where(here, jnp.take_along_axis(near[at], spot, axis=1), other))
        real, imag = scaled(*pair, phase[half, g, 2 * j], phase[half, g, 2 * j + 1])
        rows += [real.astype(BF16), imag.astype(BF16)]
    mixed = dot(merge[...], jnp.concatenate(rows, axis=0)).astype(BF16)
    merged[:, :, g] = mixed.reshape(CH, 2, GROUP, RA)


def invert(q, inverse, merged, image):
    part = dot(inverse[q], merged[q].reshape(2 * M, RA))
    for o in range(2):
        image[pl.ds(o * CH * RA + q, RA, stride=CH), :] = part[o * RA : (o + 1) * RA]


def focus_kernel(
    x_hbm,
    replica_hbm,
    w1_hbm,
    v2_hbm,
    v3_hbm,
    twiddle_hbm,
    w4_hbm,
    bank_hbm,
    spread_hbm,
    rate_hbm,
    width_hbm,
    migration_hbm,
    forward_hbm,
    merge_hbm,
    inverse_hbm,
    out_hbm,
    x,
    replica,
    w1,
    v2,
    v3,
    twiddle,
    w4,
    bank,
    spread,
    rate,
    width,
    migration,
    forward,
    merge,
    inverse,
    natural,
    spectrum,
    turn,
    rim,
    sent,
    held,
    matrix,
    doppler,
    bands,
    phase,
    place,
    merged,
    image,
    result,
    x_sem,
    table_sem,
    far_send,
    far_recv,
    near_send,
    near_recv,
    own_sem,
    out_sem,
):
    block = lax.axis_index("az")
    me = lax.axis_index("rg")
    px, pz, core = me // 8, (me // 2) % 4, me % 2
    above, below = (block + 1) % N_AZ, (block + N_AZ - 1) % N_AZ

    peers = [
        (px + x) % 4 * 8 + (pz + z) % 4 * 2 + (core + c) % 2
        for x, z in FAR_FIRST
        for c in range(2)
        if (x, z, c) != (0, 0, 0)
    ]

    fetches = [
        pltpu.make_async_copy(x_hbm.at[:, pl.ds(2 * n, 2)], x.at[:, pl.ds(2 * n, 2)], x_sem.at[n])
        for n in range(4)
    ]
    sources = [replica_hbm, w1_hbm, v2_hbm, v3_hbm, twiddle_hbm, w4_hbm, bank_hbm, spread_hbm]
    sources += [rate_hbm, width_hbm, migration_hbm, forward_hbm, merge_hbm, inverse_hbm]
    targets = [replica, w1, v2, v3, twiddle, w4, bank, spread]
    targets += [rate, width, migration, forward, merge, inverse]
    tables = [
        pltpu.make_async_copy(source, target, table_sem.at[n])
        for n, (source, target) in enumerate(zip(sources, targets))
    ]
    for copy in fetches[:1] + tables[:6]:
        copy.start()

    barrier = pltpu.get_barrier_semaphore()

    for target in peers:
        pl.semaphore_signal(barrier, inc=1, device_id=(block, target), device_id_type=MESH)

    for other in (above, below):
        pl.semaphore_signal(barrier, inc=1, device_id=(other, me), device_id_type=MESH)

    for copy in fetches[1:]:
        copy.start()

    own = [
        pltpu.make_async_copy(
            sent.at[me, pl.ds(low, high - low)],
            held.at[16 + me, pl.ds(low, high - low)],
            own_sem.at[n],
        )
        for n, (low, high) in enumerate(CUTS)
    ]

    def send(n):
        low, high = CUTS[n]
        units = pl.ds(low, high - low)

        for target in peers:
            pltpu.make_async_remote_copy(
                src_ref=sent.at[target, units],
                dst_ref=held.at[16 + me, units],
                send_sem=far_send.at[n],
                recv_sem=far_recv.at[n],
                device_id=(block, target),
                device_id_type=MESH,
            ).start()

        own[n].start()

    def onward(n, up):
        low, high = CUTS[n]
        units = pl.ds(low, high - low)
        return pltpu.make_async_remote_copy(
            src_ref=held.at[pl.ds(32 if up else 16, 16), units],
            dst_ref=held.at[pl.ds(0 if up else 48, 16), units],
            send_sem=near_send.at[int(up), n],
            recv_sem=near_recv.at[int(up), n],
            device_id=(above if up else below, me),
            device_id_type=MESH,
        )

    def relay(n):
        low, high = CUTS[n]
        whole = held.at[pl.ds(16, N_RG - 1), pl.ds(low, high - low)]
        pltpu.make_async_copy(whole, whole, far_recv.at[n]).wait()
        own[n].wait()

        @pl.when(block < N_AZ - 1)
        def _():
            onward(n, True).start()

        @pl.when(block > 0)
        def _():
            onward(n, False).start()

    def arrive(n):
        @pl.when(block < N_AZ - 1)
        def _():
            onward(n, False).wait_recv()

        @pl.when(block > 0)
        def _():
            onward(n, True).wait_recv()

    tables[0].wait()
    load_spectrum(replica, natural, spectrum)
    small = (w1, v2, v3, w4, twiddle)
    for n in range(4):
        fetches[n].wait()
        if n == 0:
            for copy in tables[1:6]:
                copy.wait()
        compress_pair(2 * n, n % 2, x, small, spectrum, turn, rim, sent)
        if n == 0:
            pl.semaphore_wait(barrier, N_RG + 1)
        send(n)
        if n == 0:
            for copy in tables[6:]:
                copy.start()
    for chunk in range(4, len(CUTS)):
        send(chunk)

    @pl.when(block == 0)
    def _():
        held[0:16] = jnp.zeros((16, UNITS, 8, RA), BF16)

    @pl.when(block == N_AZ - 1)
    def _():
        held[48:64] = jnp.zeros((16, UNITS, 8, RA), BF16)

    def phases(half, low, high):
        @pl.loop(low, high)
        def _(g):
            build_phases(g, half, rate, width, migration, phase, place)

    writes = [
        pltpu.make_async_copy(
            result.at[half, o],
            out_hbm.at[o, :, pl.ds(half * RA, RA)],
            out_sem.at[2 * half + o],
        )
        for half in range(2)
        for o in range(2)
    ]

    def complete(half, start=0):
        for g in range(start, BLOCKS):
            correct(g, half, matrix, doppler, bands, phase, place, merge, merged)
        for q in range(CH):
            invert(q, inverse, merged, image)

        for o in range(2):
            result[half, o] = image[o * CH * RA : (o + 1) * CH * RA, :].astype(BF16)
            writes[2 * half + o].start()

    def forward_chunk(n):
        arrive(n)
        if n == 4:
            forward_edges(held, forward, doppler)
        else:
            forward_pair(2 * (n % 5), int(n < 4), held, forward, doppler)

    relay(0)
    for copy in tables[6:11]:
        copy.wait()
    build_matrix(bank, spread, matrix)
    relay(1)
    phases(1, 0, 8)
    relay(2)
    phases(1, 8, 16)
    relay(3)
    phases(0, 0, 8)
    relay(4)
    phases(0, 8, 16)
    for copy in tables[11:]:
        copy.wait()
    relay(5)
    forward_chunk(0)
    forward_chunk(1)
    relay(6)
    forward_chunk(2)
    forward_chunk(3)
    relay(7)
    forward_chunk(4)
    for g in range(6):
        correct(g, 1, matrix, doppler, bands, phase, place, merge, merged)
    relay(8)
    complete(1, 6)
    for n in range(5, len(CUTS)):
        forward_chunk(n)
    complete(0)

    for n, (low, high) in enumerate(CUTS):
        whole = held.at[pl.ds(16, N_RG - 1), pl.ds(low, high - low)]
        pltpu.make_async_copy(whole, whole, far_send.at[n]).wait()

        @pl.when(block < N_AZ - 1)
        def _():
            onward(n, True).wait_send()

        @pl.when(block > 0)
        def _():
            onward(n, False).wait_send()

    for copy in writes:
        copy.wait()


def shards(echoes, replica, filter_bank, doppler_rate, doppler_width, migration):
    w1, v2, v3, w4, twiddle = range_tables()
    forward, inverse, merge, spread = azimuth_tables()
    operands = [echoes, replica]
    operands += [jnp.asarray(t) for t in (w1, v2, v3, twiddle, w4)]
    operands += [filter_bank.reshape(2 * CH * CH, M), jnp.asarray(spread)]
    operands += [a.reshape(1, 2 * RA) for a in (doppler_rate, doppler_width, migration)]
    operands += [jnp.asarray(t) for t in (forward, merge, inverse)]
    hbm = pl.BlockSpec(memory_space=pl.ANY)
    count = len(CUTS)
    return pl.pallas_call(
        focus_kernel,
        out_shape=jax.ShapeDtypeStruct((2, CH * RA, 2 * RA), BF16),
        in_specs=[hbm] * 15,
        out_specs=hbm,
        scratch_shapes=[
            pltpu.VMEM((2, CH, 4, R), BF16),
            *[pltpu.VMEM(o.shape, o.dtype) for o in operands[1:]],
            pltpu.VMEM((2 * RB, RA), F32),
            pltpu.VMEM((2, RB, RA), F32),
            pltpu.VMEM((2, 2, 4 * RB, RA), F32),
            pltpu.VMEM((N_RG * 8, RA), F32),
            pltpu.VMEM((N_RG, UNITS, 8, RA), BF16),
            pltpu.VMEM((2 * N_RG, UNITS, 8, RA), BF16),
            pltpu.VMEM((BLOCKS, M, M), BF16),
            pltpu.VMEM((3, BLOCKS, 2 * CH, GROUP, RA), BF16),
            pltpu.VMEM((BLOCKS, M, RA), F32),
            pltpu.VMEM((2, BLOCKS, 2 * CH, GROUP, RA), F32),
            pltpu.VMEM((2, BLOCKS, CH, GROUP, RA), jnp.int32),
            pltpu.VMEM((CH, 2, BLOCKS, GROUP, RA), BF16),
            pltpu.VMEM((2 * CH * RA, RA), F32),
            pltpu.VMEM((2, 2, CH * RA, RA), BF16),
            pltpu.SemaphoreType.DMA((4,)),
            pltpu.SemaphoreType.DMA((14,)),
            pltpu.SemaphoreType.DMA((count,)),
            pltpu.SemaphoreType.DMA((count,)),
            pltpu.SemaphoreType.DMA((2, count)),
            pltpu.SemaphoreType.DMA((2, count)),
            pltpu.SemaphoreType.DMA((count,)),
            pltpu.SemaphoreType.DMA((4,)),
        ],
        compiler_params=pltpu.CompilerParams(
            collective_id=0, has_side_effects=True, vmem_limit_bytes=60 * 2**20
        ),
        cost_estimate=pl.CostEstimate(
            flops=2 * 2_000_000_000, bytes_accessed=2**23, transcendentals=0
        ),
        name="focus",
    )(*operands)


def solution(mesh):
    placed = (P(None, None, ("az", "rg"), None), P(), P(), P("rg"), P("rg"), P("rg"))
    return jax.shard_map(
        shards, mesh=mesh, in_specs=placed, out_specs=P(None, "az", "rg"), check_vma=False
    )
```
